256 devices in a mesh: loop: 64 (over z, x_lo, y), grp: 4 (over x_hi, core).
Axes of the slice: x: 4 (x_hi: 2, x_lo: 2; x = x_hi * 2 + x_lo), y: 4, z: 8, core: 2. Of those that a mesh axis runs over, the one named last changes fastest.
Arguments:
- image_features: bfloat16 [12288, 1152], P('loop', 'grp'), may hold values from -4.6 to 4.6
- text_features: bfloat16 [12288, 1152], P(('loop', 'grp')), may hold values from -4.6 to 4.6
Outputs:
- image_grad: bfloat16 [12288, 1152], P('loop', 'grp')
- text_grad: bfloat16 [12288, 1152], P(('loop', 'grp'))
The draws below stay inside these ranges and needn't reach their ends.
All inputs are finite; a program needn't handle non-finite values.
Results may differ from the reference program's by a relative error of at most 0.007.
Values may be sent and summed in bfloat16 or wider, within the bound.
A program may use at most 128 MiB of HBM per device.

```python
import math
import jax
import jax.numpy as jnp
from jax import lax

D = 1152
BATCH = 12288


def draw_image_features(key, part):
    key = jax.random.fold_in(key, 11)
    columns = jnp.arange(D, dtype=jnp.float32) / float(D - 1)
    base = jax.random.truncated_normal(key, -4.0, 4.0, (BATCH, D), jnp.float32)
    spread = jnp.exp(columns * math.log(3.0))[None, :]
    values = 0.03 * base * spread
    return values.astype(jnp.bfloat16)


def draw_text_features(key, part):
    key = jax.random.fold_in(key, 23)
    columns = jnp.arange(D, dtype=jnp.float32) / float(D - 1)
    base = jax.random.truncated_normal(key, -4.0, 4.0, (BATCH, D), jnp.float32)
    spread = jnp.exp(columns * math.log(3.0))[None, :]
    values = 0.03 * base * spread
    return values.astype(jnp.bfloat16)


def setup_inputs(seed: int = 0) -> dict:
    keys = jax.random.split(jax.random.key(seed), 3)
    image_features = draw_image_features(jax.random.fold_in(keys[2], 71), 0)
    text_features = draw_text_features(jax.random.fold_in(keys[2], 71), 0)
    return {"image_features": image_features, "text_features": text_features}


LOGIT_SCALE = 16.0
LOGIT_BIAS = -4.0

def unit_rows(features):
    values = features.astype(jnp.float32)
    scale = lax.rsqrt(lax.optimization_barrier(jnp.sum(values * values, axis=-1, keepdims=True)) + 1e-06)
    return (values * scale, scale)

def back_norm(unit, scale, direction):
    inner = lax.optimization_barrier(jnp.sum(unit * direction, axis=-1, keepdims=True))
    return (scale * (direction - unit * inner)).astype(jnp.bfloat16)

def reference(image_features, text_features):
    image_unit, image_scale = unit_rows(image_features)
    text_unit, text_scale = unit_rows(text_features)
    image_low = image_unit.astype(jnp.bfloat16)
    text_low = text_unit.astype(jnp.bfloat16)
    block = math.gcd(BATCH, 512)
    count = BATCH // block

    def one_block(text_dir, index):
        start = (index * block).astype(jnp.int32)
        rows = lax.dynamic_slice_in_dim(image_low, start, block, 0)
        logits = LOGIT_SCALE * lax.dot_general(rows, text_low, (((1,), (1,)), ((), ())), preferred_element_type=jnp.float32) + LOGIT_BIAS
        row_ids = start + jnp.arange(block, dtype=jnp.int32)[:, None]
        col_ids = jnp.arange(BATCH, dtype=jnp.int32)[None, :]
        labels = jnp.where(row_ids == col_ids, 1.0, 0.0).astype(jnp.float32)
        coef = (LOGIT_SCALE * (jax.nn.sigmoid(logits) - labels)).astype(jnp.bfloat16)
        image_part = jnp.dot(coef, text_low, preferred_element_type=jnp.float32)
        text_dir = text_dir + lax.dot_general(coef, rows, (((0,), (0,)), ((), ())), preferred_element_type=jnp.float32)
        return (text_dir, image_part)
    text_dir, image_parts = lax.scan(one_block, jnp.zeros((BATCH, D), jnp.float32), jnp.arange(count, dtype=jnp.int32))
    image_dir = image_parts.reshape(BATCH, D)
    return (back_norm(image_unit, image_scale, image_dir), back_norm(text_unit, text_scale, text_dir))
```

```python
import jax
import jax.numpy as jnp
from jax import lax
from jax.experimental import pallas as pl
from jax.experimental.pallas import tpu as pltpu
from jax.sharding import PartitionSpec as P

LOGIT_SCALE = 16.0
LOGIT_BIAS = -4.0
BF16 = jnp.bfloat16
F32 = jnp.float32
R = 48
D = 1152
Q = 288
N = 768
PIECES = 3
PR = R // PIECES
COPIES = 256
MESH = pl.DeviceIdType.MESH
VIA_P = (0, 2)


def neighbours():
    loop = lax.axis_index("loop")
    grp = lax.axis_index("grp")
    z = loop // 8
    x = (grp // 2) * 2 + (loop // 4) % 2
    y = loop % 4
    c = grp % 2

    def dev(dz, dx, dy, flip=0):
        zz = (z + dz + 8) % 8
        xx = (x + dx + 4) % 4
        yy = (y + dy + 4) % 4
        return (zz * 8 + (xx % 2) * 4 + yy, (xx // 2) * 2 + (c + flip) % 2)

    f = 1 - 2 * c
    return {
        "zp": dev(f, 0, 0),
        "zm": dev(-f, 0, 0),
        "ap": dev(0, 1 - c, c),
        "am": dev(0, c - 1, -c),
        "bp": dev(0, c, 1 - c),
        "bm": dev(0, -c, c - 1),
        "sib": dev(0, 0, 0, 1),
        "g1": (loop, (grp + 1) % 4),
        "g2": (loop, (grp + 2) % 4),
        "g3": (loop, (grp + 3) % 4),
    }, loop, grp


def unit_of(values):
    scale = lax.rsqrt(jnp.sum(values * values, axis=-1, keepdims=True) + 1e-06)
    return values * scale, scale


def kernel(
    img, txt, oimg, otxt,
    xin, tin, ibuf, tbuf, coef, ip, tp, iscale, iunit,
    sib_out, sib_in, z_out, z_in, b_out, b_in, a_out, a_in, g_out, g_in,
    send_sems, recv_sems, local_sems,
):
    dev, loop, grp = neighbours()
    copies = {}

    def send(key, src, dst, to):
        index = len(copies)
        copy = pltpu.make_async_remote_copy(
            src_ref=src, dst_ref=dst, send_sem=send_sems.at[index],
            recv_sem=recv_sems.at[index], device_id=dev[to], device_id_type=MESH,
        )
        copy.start()
        copies[key] = copy

    def got(key):
        copies[key].wait_recv()

    own_rows = pl.ds(pl.multiple_of(grp * R, 16), R)
    load_t = pltpu.make_async_copy(txt, tin, local_sems.at[0])
    load_t.start()
    load_i = pltpu.make_async_copy(img.at[own_rows, :], xin.at[grp], local_sems.at[1])
    load_i.start()

    barrier = pltpu.get_barrier_semaphore()
    greeted = ("zp", "zm", "ap", "am", "bp", "bm", "g1", "g2", "g3")
    for name in greeted:
        pl.semaphore_signal(barrier, inc=1, device_id=dev[name], device_id_type=MESH)
    pl.semaphore_wait(barrier, len(greeted))

    for step in (1, 2, 3):
        there = (grp + step) % 4
        rows = pl.ds(pl.multiple_of(there * R, 16), R)
        send(("x", step), img.at[rows, :], xin.at[grp], "g%d" % step)

    pieces = range(PIECES)

    def rows_of(slot, piece):
        return pl.ds(slot * R + piece * PR, PR)

    load_t.wait()
    unit, tscale = unit_of(tin[...].astype(F32))
    tbuf[pl.ds(0, R), :] = unit.astype(BF16)

    def send_t(to, slot, new, piece):
        send(("t", new, piece), tbuf.at[rows_of(slot, piece), :], tbuf.at[rows_of(new, piece), :], to)

    def send_s(slot, piece):
        send(("s", slot, piece), tbuf.at[rows_of(slot, piece), :], tbuf.at[rows_of(slot + 8, piece), :], "sib")

    def send_i(to, slot, new, piece):
        send(("i", new, piece), ibuf.at[rows_of(slot, piece), :], ibuf.at[rows_of(new, piece), :], to)

    for p in pieces:
        send_t("zm", 0, 1, p)
        send_t("zp", 0, 7, p)
    for p in pieces:
        send_s(0, p)

    load_i.wait()
    for step in (1, 2, 3):
        got(("x", step))
    values = jnp.concatenate([xin[j].astype(F32) for j in range(4)], axis=1)
    unit_i, scale_i = unit_of(values)
    iscale[...] = jnp.broadcast_to(scale_i, (R, 128))
    iunit[...] = unit_i
    ibuf[pl.ds(0, R), :] = unit_i.astype(BF16)

    for p in pieces:
        send_i("am", 0, 1, p)
        send_i("ap", 0, 3, p)
    for p in pieces:
        send_i("bm", 0, 4, p)
        send_i("bp", 0, 12, p)

    def ring_t(new_m, new_p):
        for p in pieces:
            got(("t", new_m, p))
            if new_m < 4:
                send_t("zm", new_m, new_m + 1, p)
            if new_p is not None:
                got(("t", new_p, p))
                if new_p > 5:
                    send_t("zp", new_p, new_p - 1, p)
        for p in pieces:
            send_s(new_m, p)
            if new_p is not None:
                send_s(new_p, p)

    def far_b(d1):
        for p in pieces:
            if d1 in VIA_P:
                got(("i", 4 + d1, p))
                send_i("bm", 4 + d1, 8 + d1, p)
            else:
                got(("i", 12 + d1, p))
                send_i("bp", 12 + d1, 8 + d1, p)

    def near_b(d1):
        for p in pieces:
            got(("i", d1, p))
            send_i("bm", d1, 4 + d1, p)
            send_i("bp", d1, 12 + d1, p)

    ring_t(1, 7)
    for p in pieces:
        got(("i", 1, p))
        send_i("am", 1, 2, p)
        send_i("bm", 1, 5, p)
        send_i("bp", 1, 13, p)
    near_b(3)
    far_b(0)
    ring_t(2, 6)
    near_b(2)
    far_b(1)
    far_b(3)
    ring_t(3, 5)
    far_b(2)
    ring_t(4, None)
    for p in pieces:
        for slot in range(8):
            got(("s", slot, p))
        for d1 in range(4):
            got(("i", 8 + d1, p))
            if d1 in VIA_P:
                got(("i", 12 + d1, p))
            else:
                got(("i", 4 + d1, p))

    def one_tile(m, carry):
        rows = pl.ds(pl.multiple_of(m * 256, 256), 256)
        logits = LOGIT_SCALE * lax.dot_general(
            ibuf[rows, :], tbuf[...], (((1,), (1,)), ((), ())), preferred_element_type=F32
        ) + LOGIT_BIAS
        row_ids = m * 256 + lax.broadcasted_iota(jnp.int32, (256, N), 0)
        col_ids = lax.broadcasted_iota(jnp.int32, (256, N), 1)
        labels = jnp.where((row_ids == col_ids) & (row_ids < R), 1.0, 0.0)
        tile = (LOGIT_SCALE * (jax.nn.sigmoid(logits) - labels)).astype(BF16)
        coef[rows, :] = tile
        ip[rows, :] = jnp.dot(tile, tbuf[...], preferred_element_type=F32)
        return carry

    lax.fori_loop(0, 3, one_tile, 0)
    for n in range(3):
        cols = pl.ds(n * 256, 256)
        tp[cols, :] = lax.dot_general(
            coef[:, cols], ibuf[...], (((0,), (0,)), ((), ())), preferred_element_type=F32
        )

    for k in (4, 5, 3, 6, 2, 7, 1, 0):
        sib_out[pl.ds(k * R, R), :] = tp[pl.ds((8 + k) * R, R), :].astype(BF16)
        for p in pieces:
            rows = rows_of(k, p)
            send(("so", k, p), sib_out.at[rows, :], sib_in.at[rows, :], "sib")

    def send_b(to, slot, new, piece):
        rows = rows_of(slot, piece)
        send(("bo", slot, piece), b_out.at[rows, :], b_in.at[rows_of(new, piece), :], to)

    def b_first(d1):
        for p in pieces:
            rows = rows_of(8 + d1, p)
            b_out[rows, :] = ip[rows, :].astype(BF16)
            if d1 in VIA_P:
                send_b("bp", 8 + d1, 4 + d1, p)
            else:
                send_b("bm", 8 + d1, 12 + d1, p)

    def b_direct(d1):
        for p in pieces:
            slot = 12 + d1 if d1 in VIA_P else 4 + d1
            rows = rows_of(slot, p)
            b_out[rows, :] = ip[rows, :].astype(BF16)
            if d1 in VIA_P:
                send_b("bm", slot, d1, p)
            else:
                send_b("bp", slot, 8 + d1, p)

    def b_second(d1):
        for p in pieces:
            slot = 4 + d1 if d1 in VIA_P else 12 + d1
            rows = rows_of(slot, p)
            got(("bo", 8 + d1, p))
            b_out[rows, :] = (ip[rows, :] + b_in[rows, :].astype(F32)).astype(BF16)
            if d1 in VIA_P:
                send_b("bp", slot, 8 + d1, p)
            else:
                send_b("bm", slot, d1, p)

    def b_sum(d1, p):
        got(("bo", 4 + d1, p))
        got(("bo", 12 + d1, p))
        near = rows_of(d1, p)
        far = rows_of(8 + d1, p)
        return ip[near, :] + b_in[near, :].astype(F32) + b_in[far, :].astype(F32)

    def z_first(k, to, new):
        for p in pieces:
            rows = rows_of(k, p)
            got(("so", k, p))
            total = tp[rows, :] + sib_in[rows, :].astype(F32)
            if k not in (4, 5):
                got(("zo", k + 1 if k < 4 else k - 1, p))
                total = total + z_in[rows, :].astype(F32)
            z_out[rows, :] = total.astype(BF16)
            send(("zo", k, p), z_out.at[rows, :], z_in.at[rows_of(new, p), :], to)

    for d1 in (2, 1, 3, 0):
        b_first(d1)
    z_first(4, "zp", 3)
    z_first(5, "zm", 6)
    for d1 in (2, 1, 3, 0):
        b_direct(d1)
    z_first(3, "zp", 2)
    for d1 in (2, 1):
        b_second(d1)
    z_first(6, "zm", 7)
    for d1 in (3, 0):
        b_second(d1)
    z_first(2, "zp", 1)

    def send_a(to, slot, new, total, p):
        rows = rows_of(slot, p)
        a_out[rows, :] = total.astype(BF16)
        send(("ao", slot, p), a_out.at[rows, :], a_in.at[rows_of(new, p), :], to)

    for p in pieces:
        send_a("ap", 2, 1, b_sum(2, p), p)
    z_first(7, "zm", 4)
    for p in pieces:
        send_a("am", 3, 0, b_sum(3, p), p)
    z_first(1, "zp", 0)
    for p in pieces:
        total = b_sum(1, p)
        got(("ao", 2, p))
        send_a("ap", 1, 2, total + a_in[rows_of(1, p), :].astype(F32), p)
    for p in pieces:
        total = b_sum(0, p)
        got(("ao", 3, p))
        total = total + a_in[rows_of(0, p), :].astype(F32)
        got(("ao", 1, p))
        total = total + a_in[rows_of(2, p), :].astype(F32)
        ip[rows_of(0, p), :] = total

    def back_norm(unit_rows, scale, direction):
        inner = jnp.sum(unit_rows * direction, axis=-1, keepdims=True)
        return scale * (direction - unit_rows * inner)

    image_grad = back_norm(iunit[...], iscale[:, :1], ip[pl.ds(0, R), :])
    for j in range(4):
        g_out[j] = image_grad[:, j * Q:(j + 1) * Q].astype(BF16)
    for step in (1, 2, 3):
        send(("g", step), g_out.at[(grp + step) % 4], g_in.at[grp], "g%d" % step)
    keep = pltpu.make_async_copy(g_out.at[grp], g_in.at[grp], local_sems.at[2])
    keep.start()

    for p in pieces:
        got(("so", 0, p))
        got(("zo", 1, p))
        got(("zo", 7, p))
    own = pl.ds(0, R)
    direction = tp[own, :] + sib_in[own, :].astype(F32)
    direction = direction + z_in[own, :].astype(F32) + z_in[pl.ds(4 * R, R), :].astype(F32)
    text_unit, text_scale = unit_of(tin[...].astype(F32))
    otxt[...] = back_norm(text_unit, text_scale, direction).astype(BF16)

    keep.wait()
    for step in (1, 2, 3):
        got(("g", step))
    for j in range(4):
        oimg[pl.ds(j * R, R), :] = g_in[j]
    for copy in copies.values():
        copy.wait_send()


def on_device(image_features, text_features):
    vmem = pltpu.VMEM
    return pl.pallas_call(
        kernel,
        out_shape=(
            jax.ShapeDtypeStruct((4 * R, Q), BF16),
            jax.ShapeDtypeStruct((R, D), BF16),
        ),
        in_specs=[pl.BlockSpec(memory_space=pl.ANY)] * 2,
        out_specs=(pl.BlockSpec(memory_space=vmem), pl.BlockSpec(memory_space=vmem)),
        scratch_shapes=[
            vmem((4, R, Q), BF16),
            vmem((R, D), BF16),
            vmem((N, D), BF16),
            vmem((N, D), BF16),
            vmem((N, N), BF16),
            vmem((N, D), F32),
            vmem((N, D), F32),
            vmem((R, 128), F32),
            vmem((R, D), F32),
            vmem((8 * R, D), BF16),
            vmem((8 * R, D), BF16),
            vmem((8 * R, D), BF16),
            vmem((8 * R, D), BF16),
            vmem((N, D), BF16),
            vmem((N, D), BF16),
            vmem((4 * R, D), BF16),
            vmem((4 * R, D), BF16),
            vmem((4, R, Q), BF16),
            vmem((4, R, Q), BF16),
            pltpu.SemaphoreType.DMA((COPIES,)),
            pltpu.SemaphoreType.DMA((COPIES,)),
            pltpu.SemaphoreType.DMA((4,)),
        ],
        compiler_params=pltpu.CompilerParams(
            collective_id=0, has_side_effects=True, vmem_limit_bytes=50 * 1024 * 1024
        ),
        cost_estimate=pl.CostEstimate(
            flops=6 * N * N * D, bytes_accessed=8 * R * D, transcendentals=N * N
        ),
    )(image_features, text_features)


def solution(mesh):
    placed = (P("loop", "grp"), P(("loop", "grp"), None))
    return jax.shard_map(
        on_device, mesh=mesh, in_specs=placed, out_specs=placed, check_vma=False
    )
```

```python
import jax
import jax.numpy as jnp
from jax import lax
from jax.experimental import pallas as pl
from jax.experimental.pallas import tpu as pltpu
from jax.sharding import PartitionSpec as P

LOGIT_SCALE = 16.0
LOGIT_BIAS = -4.0
BF16 = jnp.bfloat16
F32 = jnp.float32
R = 48
D = 1152
Q = 288
N = 768
PIECES = 3
PR = R // PIECES
SENDS = 9
RECVS = 70
GREETED = ("zp", "zm", "ap", "am", "bp", "bm", "y2", "g1", "g2", "g3")
MESH = pl.DeviceIdType.MESH
VIA_P = (0, 2)


def neighbours():
    loop = lax.axis_index("loop")
    grp = lax.axis_index("grp")
    z = loop // 8
    x = (grp // 2) * 2 + (loop // 4) % 2
    y = loop % 4
    c = grp % 2

    def dev(dz, dx, dy, flip=0):
        zz = (z + dz + 8) % 8
        xx = (x + dx + 4) % 4
        yy = (y + dy + 4) % 4
        return (zz * 8 + (xx % 2) * 4 + yy, (xx // 2) * 2 + (c + flip) % 2)

    f = 1 - 2 * c
    return {
        "zp": dev(f, 0, 0),
        "zm": dev(-f, 0, 0),
        "ap": dev(0, 1 - c, c),
        "am": dev(0, c - 1, -c),
        "bp": dev(0, c, 1 - c),
        "bm": dev(0, -c, c - 1),
        "a2": dev(0, 2 - 2 * c, 2 * c),
        "b2": dev(0, 2 * c, 2 - 2 * c),
        "y2": dev(0, 0, 2),
        "sib": dev(0, 0, 0, 1),
        "g1": (loop, (grp + 1) % 4),
        "g2": (loop, (grp + 2) % 4),
        "g3": (loop, (grp + 3) % 4),
    }, loop, grp


def unit_of(values):
    scale = lax.rsqrt(jnp.sum(values * values, axis=-1, keepdims=True) + 1e-06)
    return values * scale, scale


def kernel(
    img, txt, oimg, otxt,
    xin, tin, ibuf, tbuf, coef, ip, tp, iscale, iunit,
    sib_out, sib_in, z_out, z_in, b_out, b_in, a_out, a_in, g_out, g_in,
    send_sems, recv_sems, local_sems,
):
    dev, loop, grp = neighbours()
    send_ids = {}
    recv_ids = {}

    def copy_of(kind, key, src, dst, to):
        out = send_ids.setdefault(kind, len(send_ids))
        arrive = recv_ids.setdefault(key, len(recv_ids))
        return pltpu.make_async_remote_copy(
            src_ref=src, dst_ref=dst, send_sem=send_sems.at[out],
            recv_sem=recv_sems.at[arrive], device_id=dev[to], device_id_type=MESH,
        )

    def got(key, ref):
        pltpu.make_async_copy(ref, ref, recv_sems.at[recv_ids[key]]).wait()

    def left(kind, ref):
        pltpu.make_async_copy(ref, ref, send_sems.at[send_ids[kind]]).wait()

    def blocks(slot, count=1):
        return pl.ds(slot * R, count * R)

    def rows_of(slot, piece):
        return pl.ds(slot * R + piece * PR, PR)

    pieces = range(PIECES)
    own_rows = pl.ds(pl.multiple_of(grp * R, 16), R)
    load_t = pltpu.make_async_copy(txt, tin, local_sems.at[0])
    load_t.start()
    load_i = pltpu.make_async_copy(img.at[own_rows, :], xin.at[grp], local_sems.at[1])
    load_i.start()

    barrier = pltpu.get_barrier_semaphore()
    for name in GREETED:
        pl.semaphore_signal(barrier, inc=1, device_id=dev[name], device_id_type=MESH)
    load_t.wait()
    unit, tscale = unit_of(tin[...].astype(F32))
    tbuf[blocks(0), :] = unit.astype(BF16)
    load_i.wait()
    pl.semaphore_wait(barrier, len(GREETED))

    for step in (1, 2, 3):
        there = (grp + step) % 4
        rows = pl.ds(pl.multiple_of(there * R, 16), R)
        copy_of("x", "x", img.at[rows, :], xin.at[grp], "g%d" % step).start()

    def send_t(to, slot, new, piece):
        key = ("t", new) if new in (4, 5) else ("t", new, piece)
        copy_of("t", key, tbuf.at[rows_of(slot, piece), :], tbuf.at[rows_of(new, piece), :], to).start()

    def send_s(slot):
        copy_of("s", "s", tbuf.at[blocks(slot), :], tbuf.at[blocks(slot + 8), :], "sib").start()

    for p in pieces:
        send_t("zm", 0, 1, p)
        send_t("zp", 0, 7, p)
    send_s(0)

    got("x", xin.at[pl.ds(0, 3)])
    values = jnp.concatenate([xin[j].astype(F32) for j in range(4)], axis=1)
    unit_i, scale_i = unit_of(values)
    ibuf[blocks(0), :] = unit_i.astype(BF16)

    def send_i(to, slot, new):
        copy_of("i", ("i", new), ibuf.at[blocks(slot), :], ibuf.at[blocks(new), :], to).start()

    def send_ip(to, slot, new, piece):
        copy_of(
            "i", ("i", new, piece), ibuf.at[rows_of(slot, piece), :], ibuf.at[rows_of(new, piece), :], to
        ).start()

    def send_far(to, slot, new, piece):
        copy_of(
            "i", "far", ibuf.at[rows_of(slot, piece), :], ibuf.at[rows_of(new, piece), :], to
        ).start()

    def near_b(d1):
        if d1 in VIA_P:
            for p in pieces:
                send_ip("bm", d1, 4 + d1, p)
            send_i("bp", d1, 12 + d1)
        else:
            for p in pieces:
                send_ip("bp", d1, 12 + d1, p)
            send_i("bm", d1, 4 + d1)

    def far_b(d1):
        for p in pieces:
            slot = 4 + d1 if d1 in VIA_P else 12 + d1
            got(("i", slot, p), ibuf.at[rows_of(slot, p), :])
            send_far("bm" if d1 in VIA_P else "bp", slot, 8 + d1, p)

    send_i("am", 0, 1)
    send_i("ap", 0, 3)
    send_i("a2", 0, 2)
    near_b(0)
    iscale[...] = jnp.broadcast_to(scale_i, (R, 128))
    iunit[...] = unit_i

    def ring_t(new_m, new_p):
        for p in pieces:
            got(("t", new_m, p), tbuf.at[rows_of(new_m, p), :])
            send_t("zm", new_m, new_m + 1, p)
            if new_p > 5:
                got(("t", new_p, p), tbuf.at[rows_of(new_p, p), :])
                send_t("zp", new_p, new_p - 1, p)
        send_s(new_m)
        if new_p == 5:
            got(("t", 5), tbuf.at[blocks(5), :])
        send_s(new_p)

    ring_t(1, 7)
    ring_t(2, 6)
    for d1 in (1, 3):
        got(("i", d1), ibuf.at[blocks(d1), :])
        near_b(d1)
    far_b(0)
    got(("i", 2), ibuf.at[blocks(2), :])
    near_b(2)
    ring_t(3, 5)
    far_b(1)
    far_b(3)
    got(("t", 4), tbuf.at[blocks(4), :])
    send_s(4)
    far_b(2)
    got("s", tbuf.at[blocks(8, 8), :])

    def coef_of(slot, count):
        rows = blocks(slot, count)
        logits = LOGIT_SCALE * lax.dot_general(
            ibuf[rows, :], tbuf[...], (((1,), (1,)), ((), ())), preferred_element_type=F32
        ) + LOGIT_BIAS
        chance = jax.nn.sigmoid(logits)
        if slot == 0:
            row_ids = lax.broadcasted_iota(jnp.int32, chance.shape, 0)
            col_ids = lax.broadcasted_iota(jnp.int32, chance.shape, 1)
            chance = chance - jnp.where((row_ids == col_ids) & (row_ids < R), 1.0, 0.0)
        coef[rows, :] = (LOGIT_SCALE * chance).astype(BF16)

    def image_sums(slot, count):
        rows = blocks(slot, count)
        ip[rows, :] = jnp.dot(coef[rows, :], tbuf[...], preferred_element_type=F32)

    def text_sums(slot, count, cols):
        rows = blocks(slot, count)
        return lax.dot_general(
            coef[rows, cols], ibuf[rows, :], (((0,), (0,)), ((), ())), preferred_element_type=F32
        )

    def send_b(slot, d1):
        rows = blocks(slot)
        b_out[rows, :] = ip[rows, :].astype(BF16)
        to = {1: "bp", 2: "b2", 3: "bm"}[slot // 4]
        copy_of("bo", ("bo", d1), b_out.at[rows, :], b_in.at[rows, :], to).start()

    coef_of(0, 4)
    for d1 in range(4):
        if d1 in VIA_P:
            got(("i", 12 + d1), ibuf.at[blocks(12 + d1), :])
        else:
            got(("i", 4 + d1), ibuf.at[blocks(4 + d1), :])
    coef_of(4, 4)
    image_sums(4, 4)
    for d1 in (2, 1, 3, 0):
        send_b(4 + d1, d1)
    coef_of(12, 4)
    image_sums(12, 4)
    for d1 in (2, 1, 3, 0):
        send_b(12 + d1, d1)
    thirds = [pl.ds(n * 256, 256) for n in range(3)]
    for cols in thirds:
        tp[cols, :] = text_sums(0, 8, cols) + text_sums(12, 4, cols)
    image_sums(0, 4)

    got("far", ibuf.at[blocks(8, 4), :])
    coef_of(8, 4)

    def send_so(k):
        rows = blocks(k)
        sib_out[rows, :] = tp[blocks(8 + k), :].astype(BF16)
        copy_of("so", ("so", k), sib_out.at[rows, :], sib_in.at[rows, :], "sib").start()

    for cols in (thirds[2], thirds[1], thirds[0]):
        tp[cols, :] += text_sums(8, 4, cols)
    for k in (4, 5, 3, 6, 2, 7, 1, 0):
        send_so(k)
    image_sums(8, 4)
    for d1 in (2, 1, 3, 0):
        send_b(8 + d1, d1)

    def b_sum(d1):
        got(("bo", d1), b_in.at[blocks(0, 3), :])
        total = ip[blocks(d1), :]
        for d2 in (1, 2, 3):
            total = total + b_in[blocks(4 * d2 + d1), :].astype(F32)
        return total

    def z_pass(k, to, new):
        got(("so", k), sib_in.at[blocks(k), :])
        for p in pieces:
            rows = rows_of(k, p)
            total = tp[rows, :] + sib_in[rows, :].astype(F32)
            if k not in (4, 5):
                got(("zo", k, p), z_in.at[rows, :])
                total = total + z_in[rows, :].astype(F32)
            z_out[rows, :] = total.astype(BF16)
            key = ("zo", new) if new in (0, 8) else ("zo", new, p)
            slot = 4 if new == 8 else new
            copy_of("zo", key, z_out.at[rows, :], z_in.at[rows_of(slot, p), :], to).start()

    def send_a(d1, to):
        rows = blocks(d1)
        a_out[rows, :] = b_sum(d1).astype(BF16)
        copy_of("ao", "ao", a_out.at[rows, :], a_in.at[rows, :], to).start()

    z_pass(4, "zp", 3)
    z_pass(5, "zm", 6)
    z_pass(3, "zp", 2)
    z_pass(6, "zm", 7)
    send_a(2, "a2")
    z_pass(2, "zp", 1)
    z_pass(7, "zm", 8)
    send_a(1, "ap")
    send_a(3, "am")
    z_pass(1, "zp", 0)

    def back_norm(unit_rows, scale, direction):
        inner = jnp.sum(unit_rows * direction, axis=-1, keepdims=True)
        return scale * (direction - unit_rows * inner)

    total = b_sum(0)
    got("ao", a_in.at[blocks(0, 3), :])
    for d1 in (1, 2, 3):
        total = total + a_in[blocks(d1), :].astype(F32)
    image_grad = back_norm(iunit[...], iscale[:, :1], total)
    for j in range(4):
        g_out[j] = image_grad[:, j * Q:(j + 1) * Q].astype(BF16)
    for step in (1, 2, 3):
        copy_of("g", "g", g_out.at[(grp + step) % 4], g_in.at[grp], "g%d" % step).start()
    keep = pltpu.make_async_copy(g_out.at[grp], g_in.at[grp], local_sems.at[2])
    keep.start()

    got(("so", 0), sib_in.at[blocks(0), :])
    got(("zo", 0), z_in.at[blocks(0), :])
    got(("zo", 8), z_in.at[blocks(4), :])
    direction = tp[blocks(0), :] + sib_in[blocks(0), :].astype(F32)
    direction = direction + z_in[blocks(0), :].astype(F32) + z_in[blocks(4), :].astype(F32)
    text_unit, text_scale = unit_of(tin[...].astype(F32))
    otxt[...] = back_norm(text_unit, text_scale, direction).astype(BF16)

    left("x", xin.at[pl.ds(0, 3)])
    left("t", tbuf.at[blocks(0, 7), :])
    left("s", tbuf.at[blocks(0, 8), :])
    left("i", ibuf.at[blocks(0, 15), :])
    left("so", sib_out)
    left("bo", b_out.at[blocks(0, 12), :])
    left("zo", z_out.at[blocks(0, 7), :])
    left("ao", a_out.at[blocks(0, 3), :])
    keep.wait()
    got("g", g_in.at[pl.ds(0, 3)])
    for j in range(4):
        oimg[pl.ds(j * R, R), :] = g_in[j]
    left("g", g_out.at[pl.ds(0, 3)])
    assert (len(send_ids), len(recv_ids)) == (SENDS, RECVS), (len(send_ids), len(recv_ids))


def on_device(image_features, text_features):
    vmem = pltpu.VMEM
    return pl.pallas_call(
        kernel,
        out_shape=(
            jax.ShapeDtypeStruct((4 * R, Q), BF16),
            jax.ShapeDtypeStruct((R, D), BF16),
        ),
        in_specs=[pl.BlockSpec(memory_space=pl.ANY)] * 2,
        out_specs=(pl.BlockSpec(memory_space=vmem), pl.BlockSpec(memory_space=vmem)),
        scratch_shapes=[
            vmem((4, R, Q), BF16),
            vmem((R, D), BF16),
            vmem((N, D), BF16),
            vmem((N, D), BF16),
            vmem((N, N), BF16),
            vmem((N, D), F32),
            vmem((N, D), F32),
            vmem((R, 128), F32),
            vmem((R, D), F32),
            vmem((8 * R, D), BF16),
            vmem((8 * R, D), BF16),
            vmem((8 * R, D), BF16),
            vmem((8 * R, D), BF16),
            vmem((N, D), BF16),
            vmem((N, D), BF16),
            vmem((4 * R, D), BF16),
            vmem((4 * R, D), BF16),
            vmem((4, R, Q), BF16),
            vmem((4, R, Q), BF16),
            pltpu.SemaphoreType.DMA((SENDS,)),
            pltpu.SemaphoreType.DMA((RECVS,)),
            pltpu.SemaphoreType.DMA((3,)),
        ],
        compiler_params=pltpu.CompilerParams(
            collective_id=0, has_side_effects=True, vmem_limit_bytes=60 * 1024 * 1024
        ),
        cost_estimate=pl.CostEstimate(
            flops=6 * N * N * D, bytes_accessed=8 * R * D, transcendentals=N * N
        ),
    )(image_features, text_features)


def solution(mesh):
    placed = (P("loop", "grp"), P(("loop", "grp"), None))
    return jax.shard_map(
        on_device, mesh=mesh, in_specs=placed, out_specs=placed, check_vma=False
    )
```

```python
import jax
import jax.numpy as jnp
from jax import lax
from jax.experimental import pallas as pl
from jax.experimental.pallas import tpu as pltpu
from jax.sharding import PartitionSpec as P

LOGIT_SCALE = 16.0
LOGIT_BIAS = -4.0
BF16 = jnp.bfloat16
F32 = jnp.float32
H = 96
R = 48
D = 1152
Q = 288
N = 768
PIECES = 3
PR = R // PIECES
SENDS = 10
RECVS = 64
GREETED = ("zp", "zm", "zp2", "zm2", "ap", "am", "bp", "bm", "y2", "g1", "g2", "g3")
MESH = pl.DeviceIdType.MESH
FORWARD = (0, 1, 3, 2)
OWN = {0: 0, 1: 1, 7: 2, 2: 3, 6: 4, 3: 10, 5: 11, 4: 12}
OTHER = {k: place + (5 if place < 5 else 3) for k, place in OWN.items()}
EARLY = 10 * R
LATE = N - EARLY
VIA_P = (0, 2)


def neighbours():
    loop = lax.axis_index("loop")
    grp = lax.axis_index("grp")
    z = loop // 8
    x = (grp // 2) * 2 + (loop // 4) % 2
    y = loop % 4
    c = grp % 2

    def dev(dz, dx, dy, flip=0):
        zz = (z + dz + 8) % 8
        xx = (x + dx + 4) % 4
        yy = (y + dy + 4) % 4
        return (zz * 8 + (xx % 2) * 4 + yy, (xx // 2) * 2 + (c + flip) % 2)

    f = 1 - 2 * c
    return {
        "zp": dev(f, 0, 0),
        "zm": dev(-f, 0, 0),
        "zp2": dev(2 * f, 0, 0),
        "zm2": dev(-2 * f, 0, 0),
        "ap": dev(0, 1 - c, c),
        "am": dev(0, c - 1, -c),
        "bp": dev(0, c, 1 - c),
        "bm": dev(0, -c, c - 1),
        "a2": dev(0, 2 - 2 * c, 2 * c),
        "b2": dev(0, 2 * c, 2 - 2 * c),
        "y2": dev(0, 0, 2),
        "sib": dev(0, 0, 0, 1),
        "g1": (loop, (grp + 1) % 4),
        "g2": (loop, (grp + 2) % 4),
        "g3": (loop, (grp + 3) % 4),
    }, grp, x, c


def unit_of(values):
    scale = lax.rsqrt(jnp.sum(values * values, axis=-1, keepdims=True) + 1e-06)
    return values * scale, scale


def permuted(values):
    mains = [values[:, q * Q:q * Q + 256] for q in range(4)]
    return jnp.concatenate(mains + [values[:, q * Q + 256:(q + 1) * Q] for q in range(4)], axis=1)


def quarter(values, q):
    return jnp.concatenate(
        [values[:, q * 256:(q + 1) * 256], values[:, 1024 + q * 32:1024 + (q + 1) * 32]], axis=1
    )


def kernel(
    img, txt, oimg, otxt,
    ximg, xrem, srem, rmain, rrem, tin, ibuf, tbuf, coef_early, coef_late, ip, tp,
    sib_out, sib_in, z_out, z_in, b_out, b_in, a_out, a_in, g_out, g_in,
    send_sems, recv_sems, local_sems,
):
    dev, grp, x, c = neighbours()
    xh = x // 2
    send_ids = {}
    recv_ids = {}

    def copy_of(kind, key, src, dst, to):
        out = send_ids.setdefault(kind, len(send_ids))
        arrive = recv_ids.setdefault(key, len(recv_ids))
        return pltpu.make_async_remote_copy(
            src_ref=src, dst_ref=dst, send_sem=send_sems.at[out],
            recv_sem=recv_sems.at[arrive], device_id=dev[to], device_id_type=MESH,
        )

    def got(key, ref):
        pltpu.make_async_copy(ref, ref, recv_sems.at[recv_ids[key]]).wait()

    def left(kind, ref):
        pltpu.make_async_copy(ref, ref, send_sems.at[send_ids[kind]]).wait()

    def blocks(slot, count=1):
        return pl.ds(slot * R, count * R)

    def rows_of(slot, piece):
        return pl.ds(slot * R + piece * PR, PR)

    pieces = range(PIECES)
    load_t = pltpu.make_async_copy(txt, tin, local_sems.at[0])
    load_t.start()
    load_i = pltpu.make_async_copy(img, ximg, local_sems.at[1])
    load_i.start()

    barrier = pltpu.get_barrier_semaphore()
    for name in GREETED:
        pl.semaphore_signal(barrier, inc=1, device_id=dev[name], device_id_type=MESH)
    load_t.wait()
    unit, tscale = unit_of(permuted(tin[...].astype(F32)))
    tbuf[blocks(0), :] = unit.astype(BF16)
    load_i.wait()

    def rest_of(half):
        rest = ximg[pl.ds(pl.multiple_of(half * H, 32), H), 256:].astype(F32)
        low, high = rest[:R], rest[R:]
        gap = jnp.zeros_like(low)
        return jnp.where(
            c == 0,
            jnp.concatenate([low, gap, high, gap], axis=1),
            jnp.concatenate([gap, low, gap, high], axis=1),
        )

    xrem[...] = rest_of(1 - c).astype(BF16)
    rest_here = rest_of(c)
    there = pl.ds(pl.multiple_of((1 - c) * H, 32), H)
    here = pl.ds(pl.multiple_of(c * H, 32), H)
    rmain[grp, pl.ds(4 * H, H), :] = ximg[here, :256]
    pl.semaphore_wait(barrier, len(GREETED))

    copy_of("x", "x", ximg.at[there, pl.ds(0, 256)], rmain.at[grp, pl.ds(4 * H, H), :], "sib").start()
    copy_of("y", "x", xrem, srem, "sib").start()

    def send_t(to, slot, new, piece):
        key = ("t", new) if new in (3, 4, 5) else ("t", new, piece)
        src, dst = rows_of(OWN[slot], piece), rows_of(OWN[new], piece)
        copy_of("t", key, tbuf.at[src, :], tbuf.at[dst, :], to).start()

    def send_s(slot):
        key = "s late" if slot in (3, 5, 4) else "s early"
        src, dst = blocks(OWN[slot]), blocks(OTHER[slot])
        copy_of("s", key, tbuf.at[src, :], tbuf.at[dst, :], "sib").start()

    for p in pieces:
        send_t("zm", 0, 1, p)
        send_t("zp", 0, 7, p)
    send_s(0)

    def slot_of(d1, d2):
        return 4 * (1 - d2 % 2) + (1 - c) * ((d2 // 2) * 2 + d1 % 2) + c * d1

    def half_of(d1, d2):
        return ((x + (1 - c) * d1 + c * d2) % 4) // 2

    def send_i(to, source, target, key):
        half = half_of(*source)
        quarters = pl.ds(2 * half, 2)
        came, goes = slot_of(*source), slot_of(*target)
        src = pl.ds(pl.multiple_of(came * H, 32), H)
        dst = pl.ds(pl.multiple_of(goes * H, 32), H)
        copy_of("i", key, rmain.at[quarters, src, :], rmain.at[quarters, dst, :], to).start()
        src = pl.ds(pl.multiple_of(came * R, 16), R)
        dst = pl.ds(pl.multiple_of(goes * R, 16), R)
        copy_of("i", key, rrem.at[half, src, :], rrem.at[half, dst, :], to).start()

    def got_i(key):
        got(key, tbuf.at[blocks(0), :])

    def near_b(d1):
        send_i("bm", (d1, 0), (d1, 1), ("i", d1, 1))
        send_i("bp", (d1, 0), (d1, 3), ("i", d1, 3))
        if d1 not in FORWARD:
            send_i("b2", (d1, 0), (d1, 2), ("i", d1, 2))

    def far_b(d1):
        if d1 in VIA_P:
            got_i(("i", d1, 1))
            send_i("bm", (d1, 1), (d1, 2), ("i", d1, 2))
        else:
            got_i(("i", d1, 3))
            send_i("bp", (d1, 3), (d1, 2), ("i", d1, 2))

    got("x", rrem.at[0, pl.ds(0, 5 * R), :])
    rrem[xh, pl.ds(4 * R, R), :] = (rest_here + srem[...].astype(F32)).astype(BF16)
    send_i("am", (0, 0), (1, 0), ("i", 1, 0))
    send_i("ap", (0, 0), (3, 0), ("i", 3, 0))
    send_i("a2", (0, 0), (2, 0), ("i", 2, 0))
    near_b(0)

    def ring_t(new_m, new_p):
        for p in pieces:
            got(("t", new_m, p), tbuf.at[rows_of(OWN[new_m], p), :])
            send_t("zm", new_m, new_m + 1, p)
            if new_p == 6:
                send_t("zm2", 2, 4, p)
            got(("t", new_p, p), tbuf.at[rows_of(OWN[new_p], p), :])
            send_t("zp", new_p, new_p - 1, p)
        send_s(new_m)
        send_s(new_p)

    ring_t(1, 7)
    for d1 in (1, 3):
        got_i(("i", d1, 0))
        near_b(d1)
    got_i(("i", 2, 0))
    near_b(2)
    ring_t(2, 6)
    for d1 in FORWARD:
        far_b(d1)

    def late_t(slot):
        got(("t", slot), tbuf.at[blocks(OWN[slot]), :])
        send_s(slot)

    def rests(slot):
        rows = pl.ds(pl.multiple_of(slot * R, 16), R)
        first, second = rrem[0, rows, :].astype(F32), rrem[1, rows, :].astype(F32)
        left_side = lax.broadcasted_iota(jnp.int32, first.shape, 1) < 64
        low = jnp.where(left_side, first, pltpu.roll(second, 64, 1))
        high = jnp.where(left_side, pltpu.roll(first, 64, 1), second)
        return low, high

    def normalise(slot, carry):
        rows = pl.ds(pl.multiple_of(slot * H, 32), H)
        parts = [rmain[q, rows, :].astype(F32) for q in range(4)]
        parts.append(jnp.concatenate(rests(slot), axis=0))
        squares = [jnp.sum(part * part, axis=-1, keepdims=True) for part in parts]
        scale = lax.rsqrt(sum(squares[1:], squares[0]) + 1e-06)
        for q, part in enumerate(parts):
            ibuf[rows, pl.ds(256 * q, part.shape[1])] = (part * scale).astype(BF16)
        return carry

    def normalised(slot, count):
        lax.fori_loop(slot, slot + count, normalise, 0)

    def coef_of(slot, count, part):
        store, texts = part
        rows = pl.ds(slot * H, count * H)
        logits = LOGIT_SCALE * lax.dot_general(
            ibuf[rows, :], tbuf[texts, :], (((1,), (1,)), ((), ())), preferred_element_type=F32
        ) + LOGIT_BIAS
        chance = jax.nn.sigmoid(logits)
        if slot == 4 and part is early:
            row_ids = lax.broadcasted_iota(jnp.int32, chance.shape, 0)
            col_ids = lax.broadcasted_iota(jnp.int32, chance.shape, 1)
            start = OTHER[0] * R
            own = (col_ids < R) & (row_ids == col_ids + c * R)
            other = (col_ids >= start) & (col_ids < start + R) & (row_ids == col_ids - start + (1 - c) * R)
            chance = chance - jnp.where((own | other) & (c == xh), 1.0, 0.0)
        store[rows, :] = (LOGIT_SCALE * chance).astype(BF16)

    def image_sums(slot, count, part):
        store, texts = part
        rows = pl.ds(slot * H, count * H)
        return jnp.dot(store[rows, :], tbuf[texts, :], preferred_element_type=F32)

    def text_sums(slot, count, part):
        rows = pl.ds(slot * H, count * H)
        return lax.dot_general(
            part[0][rows, :], ibuf[rows, :], (((0,), (0,)), ((), ())), preferred_element_type=F32
        )

    early = (coef_early, pl.ds(0, EARLY))
    late = (coef_late, pl.ds(EARLY, LATE))

    def part_of(d1, d2):
        start = slot_of(d1, d2) * H + half_of(d1, d2) * R
        return ip[pl.ds(pl.multiple_of(start, 16), R), :]

    def send_b(d1, d2):
        rows = blocks(4 * d2 + d1)
        b_out[rows, :] = part_of(d1, d2).astype(BF16)
        to = {1: "bp", 2: "b2", 3: "bm"}[d2]
        copy_of("bo", ("bo", d1), b_out.at[rows, :], b_in.at[rows, :], to).start()

    for d1 in range(4):
        for d2 in (1, 3):
            if d1 not in FORWARD or d2 != (1 if d1 in VIA_P else 3):
                got_i(("i", d1, d2))
    first, second, third = pl.ds(0, 4 * H), pl.ds(4 * H, 2 * H), pl.ds(6 * H, 2 * H)
    normalised(0, 4)
    got("s early", tbuf.at[blocks(0, 5), :])
    coef_of(0, 4, early)
    ip[first, :] = image_sums(0, 4, early)
    late_t(3)
    late_t(5)
    for d1 in (0, 1):
        got_i(("i", d1, 2))
    normalised(4, 2)
    coef_of(4, 2, early)
    late_t(4)
    tp[early[1], :] = text_sums(0, 6, early)
    ip[second, :] = image_sums(4, 2, early)

    got("s late", tbuf.at[blocks(0, 3), :])
    coef_of(0, 4, late)
    ip[first, :] += image_sums(0, 4, late)
    for d1 in (2, 1, 3, 0):
        for d2 in (1, 3):
            send_b(d1, d2)
    coef_of(4, 2, late)
    for d1 in (2, 3):
        got_i(("i", d1, 2))
    normalised(6, 2)
    coef_of(6, 2, late)
    coef_of(6, 2, early)

    def send_so(k):
        rows = blocks(k)
        sib_out[rows, :] = tp[blocks(OTHER[k]), :].astype(BF16)
        copy_of("so", ("so", k), sib_out.at[rows, :], sib_in.at[rows, :], "sib").start()

    tp[late[1], :] = text_sums(0, 8, late)
    for k in (4, 5, 3):
        send_so(k)
    tp[early[1], :] += text_sums(6, 2, early)
    for k in (6, 2, 7, 1, 0):
        send_so(k)
    ip[second, :] += image_sums(4, 2, late)
    ip[third, :] = image_sums(6, 2, early) + image_sums(6, 2, late)
    for d1 in (2, 1, 3, 0):
        send_b(d1, 2)

    def b_sum(d1):
        got(("bo", d1), b_in.at[blocks(0, 3), :])
        total = part_of(d1, 0)
        for d2 in (1, 2, 3):
            total = total + b_in[blocks(4 * d2 + d1), :].astype(F32)
        return total

    def z_pass(k, to, new):
        got(("so", k), sib_in.at[blocks(k), :])
        for p in pieces:
            rows = rows_of(k, p)
            total = tp[rows_of(OWN[k], p), :] + sib_in[rows, :].astype(F32)
            if k not in (4, 5):
                got(("zo", k, p), z_in.at[rows, :])
                total = total + z_in[rows, :].astype(F32)
            z_out[rows, :] = total.astype(BF16)
            key = ("zo", new) if new in (0, 8) else ("zo", new, p)
            slot = 4 if new == 8 else new
            copy_of("zo", key, z_out.at[rows, :], z_in.at[rows_of(slot, p), :], to).start()

    def send_a(d1, to):
        rows = blocks(d1)
        a_out[rows, :] = b_sum(d1).astype(BF16)
        copy_of("ao", "ao", a_out.at[rows, :], a_in.at[rows, :], to).start()

    z_pass(4, "zp", 3)
    z_pass(5, "zm", 6)
    z_pass(3, "zp", 2)
    z_pass(6, "zm", 7)
    send_a(2, "a2")
    z_pass(2, "zp", 1)
    z_pass(7, "zm", 8)
    send_a(1, "ap")
    send_a(3, "am")
    z_pass(1, "zp", 0)

    def back_norm(unit_rows, scale, direction):
        inner = jnp.sum(unit_rows * direction, axis=-1, keepdims=True)
        return scale * (direction - unit_rows * inner)

    total = b_sum(0)
    got("ao", a_in.at[blocks(0, 3), :])
    for d1 in (1, 2, 3):
        total = total + a_in[blocks(d1), :].astype(F32)
    own_rows = pl.ds(pl.multiple_of(4 * H + xh * R, 16), R)
    low, high = rests(4)
    own_parts = [rmain[q, own_rows, :].astype(F32) for q in range(4)]
    image_unit, image_scale = unit_of(jnp.concatenate(own_parts + [jnp.where(xh == 0, low, high)], axis=1))
    image_grad = back_norm(image_unit, image_scale, total)
    for j in range(4):
        g_out[j] = quarter(image_grad, j).astype(BF16)
    for step in (1, 2, 3):
        copy_of("g", "g", g_out.at[(grp + step) % 4], g_in.at[grp], "g%d" % step).start()
    keep = pltpu.make_async_copy(g_out.at[grp], g_in.at[grp], local_sems.at[2])
    keep.start()

    got(("so", 0), sib_in.at[blocks(0), :])
    got(("zo", 0), z_in.at[blocks(0), :])
    got(("zo", 8), z_in.at[blocks(4), :])
    direction = tp[blocks(0), :] + sib_in[blocks(0), :].astype(F32)
    direction = direction + z_in[blocks(0), :].astype(F32) + z_in[blocks(4), :].astype(F32)
    text_unit, text_scale = unit_of(permuted(tin[...].astype(F32)))
    text_grad = back_norm(text_unit, text_scale, direction)
    otxt[...] = jnp.concatenate([quarter(text_grad, j) for j in range(4)], axis=1).astype(BF16)

    left("x", rmain.at[0, pl.ds(0, H), :])
    left("y", xrem)
    left("t", tbuf.at[blocks(0, 7), :])
    left("s", tbuf.at[blocks(0, 8), :])
    left("i", ibuf.at[blocks(0, 15), :])
    left("so", sib_out)
    left("bo", b_out.at[blocks(0, 12), :])
    left("zo", z_out.at[blocks(0, 7), :])
    left("ao", a_out.at[blocks(0, 3), :])
    keep.wait()
    got("g", g_in.at[pl.ds(0, 3)])
    for j in range(4):
        oimg[pl.ds((j % 2) * H + (j // 2) * R, R), :] = g_in[j]
    left("g", g_out.at[pl.ds(0, 3)])
    assert (len(send_ids), len(recv_ids)) == (SENDS, RECVS), (len(send_ids), len(recv_ids))


def on_device(image_features, text_features):
    vmem = pltpu.VMEM
    return pl.pallas_call(
        kernel,
        out_shape=(
            jax.ShapeDtypeStruct((4 * R, Q), BF16),
            jax.ShapeDtypeStruct((R, D), BF16),
        ),
        in_specs=[pl.BlockSpec(memory_space=pl.ANY)] * 2,
        out_specs=(pl.BlockSpec(memory_space=vmem), pl.BlockSpec(memory_space=vmem)),
        scratch_shapes=[
            vmem((4 * R, Q), BF16),
            vmem((R, 128), BF16),
            vmem((R, 128), BF16),
            vmem((4, N, 256), BF16),
            vmem((2, N // 2, 128), BF16),
            vmem((R, D), BF16),
            vmem((N, D), BF16),
            vmem((N, D), BF16),
            vmem((N, EARLY), BF16),
            vmem((N, LATE), BF16),
            vmem((N, D), F32),
            vmem((N, D), F32),
            vmem((8 * R, D), BF16),
            vmem((8 * R, D), BF16),
            vmem((8 * R, D), BF16),
            vmem((8 * R, D), BF16),
            vmem((N, D), BF16),
            vmem((N, D), BF16),
            vmem((4 * R, D), BF16),
            vmem((4 * R, D), BF16),
            vmem((4, R, Q), BF16),
            vmem((4, R, Q), BF16),
            pltpu.SemaphoreType.DMA((SENDS,)),
            pltpu.SemaphoreType.DMA((RECVS,)),
            pltpu.SemaphoreType.DMA((3,)),
        ],
        compiler_params=pltpu.CompilerParams(
            collective_id=0, has_side_effects=True, vmem_limit_bytes=60 * 1024 * 1024
        ),
        cost_estimate=pl.CostEstimate(
            flops=6 * N * N * D, bytes_accessed=8 * R * D, transcendentals=N * N
        ),
    )(image_features, text_features)


def solution(mesh):
    placed = (P("loop", "grp"), P(("loop", "grp"), None))
    return jax.shard_map(
        on_device, mesh=mesh, in_specs=placed, out_specs=placed, check_vma=False
    )
```

```python
import jax
import jax.numpy as jnp
from jax import lax
from jax.experimental import pallas as pl
from jax.experimental.pallas import tpu as pltpu
from jax.sharding import PartitionSpec as P

LOGIT_SCALE = 16.0
LOGIT_BIAS = -4.0
BF16 = jnp.bfloat16
F32 = jnp.float32
H = 96
R = 48
D = 1152
Q = 288
N = 768
PIECES = 3
PR = R // PIECES
SENDS = 13
RECVS = 66
GREETED = ("zp", "zm", "zp2", "zm2", "ap", "am", "bp", "bm", "x2", "y2", "sib")
MESH = pl.DeviceIdType.MESH
FORWARD = (0, 1, 3, 2)
OWN = {0: 0, 1: 1, 7: 2, 2: 3, 6: 4, 3: 10, 5: 11, 4: 12}
OTHER = {k: place + (5 if place < 5 else 3) for k, place in OWN.items()}
EARLY = 10 * R
LATE = N - EARLY
VIA_P = (0, 2)


def neighbours():
    loop = lax.axis_index("loop")
    grp = lax.axis_index("grp")
    z = loop // 8
    x = (grp // 2) * 2 + (loop // 4) % 2
    y = loop % 4
    c = grp % 2

    def dev(dz, dx, dy, flip=0):
        zz = (z + dz + 8) % 8
        xx = (x + dx + 4) % 4
        yy = (y + dy + 4) % 4
        return (zz * 8 + (xx % 2) * 4 + yy, (xx // 2) * 2 + (c + flip) % 2)

    f = 1 - 2 * c
    return {
        "zp": dev(f, 0, 0),
        "zm": dev(-f, 0, 0),
        "zp2": dev(2 * f, 0, 0),
        "zm2": dev(-2 * f, 0, 0),
        "ap": dev(0, 1 - c, c),
        "am": dev(0, c - 1, -c),
        "bp": dev(0, c, 1 - c),
        "bm": dev(0, -c, c - 1),
        "a2": dev(0, 2 - 2 * c, 2 * c),
        "b2": dev(0, 2 * c, 2 - 2 * c),
        "x2": dev(0, 2, 0),
        "y2": dev(0, 0, 2),
        "sib": dev(0, 0, 0, 1),
    }, grp, x, c


def unit_of(values):
    scale = lax.rsqrt(jnp.sum(values * values, axis=-1, keepdims=True) + 1e-06)
    return values * scale, scale


def permuted(values):
    mains = [values[:, q * Q:q * Q + 256] for q in range(4)]
    return jnp.concatenate(mains + [values[:, q * Q + 256:(q + 1) * Q] for q in range(4)], axis=1)


def quarter(values, q):
    return jnp.concatenate(
        [values[:, q * 256:(q + 1) * 256], values[:, 1024 + q * 32:1024 + (q + 1) * 32]], axis=1
    )


def kernel(
    img, txt, oimg, otxt,
    ximg, xrem, srem, rmain, rrem, tin, tunit, tscales, ibuf, tbuf, coef_early, coef_late, ip, tp,
    sib_out, sib_in, z_out, z_in, b_main, b_rest, b_main_in, b_rest_in, a_main, a_rest, a_main_in, a_rest_in,
    inner_sums, inner_slots, b_inner, b_inner_in, a_inner, a_inner_in, g_main, g_rest, g_main_in, g_rest_in,
    send_sems, recv_sems, local_sems,
):
    dev, grp, x, c = neighbours()
    xh = x // 2
    send_ids = {}
    recv_ids = {}

    def copy_of(kind, key, src, dst, to):
        out = send_ids.setdefault(kind, len(send_ids))
        arrive = recv_ids.setdefault(key, len(recv_ids))
        return pltpu.make_async_remote_copy(
            src_ref=src, dst_ref=dst, send_sem=send_sems.at[out],
            recv_sem=recv_sems.at[arrive], device_id=dev[to], device_id_type=MESH,
        )

    def got(key, ref):
        pltpu.make_async_copy(ref, ref, recv_sems.at[recv_ids[key]]).wait()

    def left(kind, ref):
        pltpu.make_async_copy(ref, ref, send_sems.at[send_ids[kind]]).wait()

    def blocks(slot, count=1):
        return pl.ds(slot * R, count * R)

    def rows_of(slot, piece):
        return pl.ds(slot * R + piece * PR, PR)

    pieces = range(PIECES)
    load_t = pltpu.make_async_copy(txt, tin, local_sems.at[0])
    load_t.start()
    load_i = pltpu.make_async_copy(img, ximg, local_sems.at[1])
    load_i.start()

    barrier = pltpu.get_barrier_semaphore()
    for name in GREETED:
        pl.semaphore_signal(barrier, inc=1, device_id=dev[name], device_id_type=MESH)
    load_t.wait()
    unit, tscale = unit_of(permuted(tin[...].astype(F32)))
    tbuf[blocks(0), :] = unit.astype(BF16)
    tunit[...] = unit
    tscales[...] = jnp.broadcast_to(tscale, (R, 128))
    inner_sums[...] = jnp.zeros_like(inner_sums)
    load_i.wait()

    def rest_of(half):
        rest = ximg[pl.ds(pl.multiple_of(half * H, 32), H), 256:].astype(F32)
        low, high = rest[:R], rest[R:]
        gap = jnp.zeros_like(low)
        return jnp.where(
            c == 0,
            jnp.concatenate([low, gap, high, gap], axis=1),
            jnp.concatenate([gap, low, gap, high], axis=1),
        )

    xrem[...] = rest_of(1 - c).astype(BF16)
    rest_here = rest_of(c)
    there = pl.ds(pl.multiple_of((1 - c) * H, 32), H)
    here = pl.ds(pl.multiple_of(c * H, 32), H)
    rmain[grp, pl.ds(4 * H, H), :] = ximg[here, :256]
    pl.semaphore_wait(barrier, len(GREETED))

    copy_of("x", "x", ximg.at[there, pl.ds(0, 256)], rmain.at[grp, pl.ds(4 * H, H), :], "sib").start()
    copy_of("y", "x", xrem, srem, "sib").start()

    def send_t(to, slot, new, piece):
        key = ("t", new) if new in (3, 4, 5) else ("t", new, piece)
        src, dst = rows_of(OWN[slot], piece), rows_of(OWN[new], piece)
        copy_of("t", key, tbuf.at[src, :], tbuf.at[dst, :], to).start()

    def send_s(slot):
        key = "s late" if slot in (3, 5, 4) else "s early"
        src, dst = blocks(OWN[slot]), blocks(OTHER[slot])
        copy_of("s", key, tbuf.at[src, :], tbuf.at[dst, :], "sib").start()

    for p in pieces:
        send_t("zm", 0, 1, p)
        send_t("zp", 0, 7, p)
    send_s(0)

    def slot_of(d1, d2):
        return 4 * (1 - d2 % 2) + (1 - c) * ((d2 // 2) * 2 + d1 % 2) + c * d1

    def half_of(d1, d2):
        return ((x + (1 - c) * d1 + c * d2) % 4) // 2

    def send_i(to, source, target, key):
        half = half_of(*source)
        quarters = pl.ds(2 * half, 2)
        came, goes = slot_of(*source), slot_of(*target)
        src = pl.ds(pl.multiple_of(came * H, 32), H)
        dst = pl.ds(pl.multiple_of(goes * H, 32), H)
        copy_of("i", key, rmain.at[quarters, src, :], rmain.at[quarters, dst, :], to).start()
        src = pl.ds(pl.multiple_of(came * R, 16), R)
        dst = pl.ds(pl.multiple_of(goes * R, 16), R)
        copy_of("i", key, rrem.at[half, src, :], rrem.at[half, dst, :], to).start()

    def got_i(key):
        got(key, tbuf.at[blocks(0), :])

    def near_b(d1):
        send_i("bm", (d1, 0), (d1, 1), ("i", d1, 1))
        send_i("bp", (d1, 0), (d1, 3), ("i", d1, 3))
        if d1 not in FORWARD:
            send_i("b2", (d1, 0), (d1, 2), ("i", d1, 2))

    def far_b(d1):
        if d1 in VIA_P:
            got_i(("i", d1, 1))
            send_i("bm", (d1, 1), (d1, 2), ("i", d1, 2))
        else:
            got_i(("i", d1, 3))
            send_i("bp", (d1, 3), (d1, 2), ("i", d1, 2))

    got("x", rrem.at[0, pl.ds(0, 5 * R), :])
    rrem[xh, pl.ds(4 * R, R), :] = (rest_here + srem[...].astype(F32)).astype(BF16)
    send_i("am", (0, 0), (1, 0), ("i", 1, 0))
    send_i("ap", (0, 0), (3, 0), ("i", 3, 0))
    send_i("a2", (0, 0), (2, 0), ("i", 2, 0))
    near_b(0)

    def ring_t(new_m, new_p):
        for p in pieces:
            got(("t", new_m, p), tbuf.at[rows_of(OWN[new_m], p), :])
            send_t("zm", new_m, new_m + 1, p)
            if new_p == 6:
                send_t("zm2", 2, 4, p)
            got(("t", new_p, p), tbuf.at[rows_of(OWN[new_p], p), :])
            send_t("zp", new_p, new_p - 1, p)
        send_s(new_m)
        send_s(new_p)

    ring_t(1, 7)
    for d1 in (1, 3):
        got_i(("i", d1, 0))
        near_b(d1)
    got_i(("i", 2, 0))
    near_b(2)
    ring_t(2, 6)
    for d1 in FORWARD:
        far_b(d1)

    def late_t(slot):
        got(("t", slot), tbuf.at[blocks(OWN[slot]), :])
        send_s(slot)

    def rests(slot):
        rows = pl.ds(pl.multiple_of(slot * R, 16), R)
        first, second = rrem[0, rows, :].astype(F32), rrem[1, rows, :].astype(F32)
        left_side = lax.broadcasted_iota(jnp.int32, first.shape, 1) < 64
        low = jnp.where(left_side, first, pltpu.roll(second, 64, 1))
        high = jnp.where(left_side, pltpu.roll(first, 64, 1), second)
        return low, high

    def normalise(slot, carry):
        rows = pl.ds(pl.multiple_of(slot * H, 32), H)
        parts = [rmain[q, rows, :].astype(F32) for q in range(4)]
        parts.append(jnp.concatenate(rests(slot), axis=0))
        squares = [jnp.sum(part * part, axis=-1, keepdims=True) for part in parts]
        scale = lax.rsqrt(sum(squares[1:], squares[0]) + 1e-06)
        for q, part in enumerate(parts):
            ibuf[rows, pl.ds(256 * q, part.shape[1])] = (part * scale).astype(BF16)
        return carry

    def normalised(slot, count):
        lax.fori_loop(slot, slot + count, normalise, 0)

    def coef_of(slot, count, part):
        store, texts = part
        rows = pl.ds(slot * H, count * H)
        logits = LOGIT_SCALE * lax.dot_general(
            ibuf[rows, :], tbuf[texts, :], (((1,), (1,)), ((), ())), preferred_element_type=F32
        ) + LOGIT_BIAS
        chance = jax.nn.sigmoid(logits)
        if slot == 4 and part is early:
            row_ids = lax.broadcasted_iota(jnp.int32, chance.shape, 0)
            col_ids = lax.broadcasted_iota(jnp.int32, chance.shape, 1)
            start = OTHER[0] * R
            own = (col_ids < R) & (row_ids == col_ids + c * R)
            other = (col_ids >= start) & (col_ids < start + R) & (row_ids == col_ids - start + (1 - c) * R)
            chance = chance - jnp.where((own | other) & (c == xh), 1.0, 0.0)
        store[rows, :] = (LOGIT_SCALE * chance).astype(BF16)

    def image_sums(slot, count, part):
        store, texts = part
        rows = pl.ds(slot * H, count * H)
        return jnp.dot(store[rows, :], tbuf[texts, :], preferred_element_type=F32)

    def text_sums(slot, count, part):
        rows = pl.ds(slot * H, count * H)
        return lax.dot_general(
            part[0][rows, :], ibuf[rows, :], (((0,), (0,)), ((), ())), preferred_element_type=F32
        )

    early = (coef_early, pl.ds(0, EARLY))
    late = (coef_late, pl.ds(EARLY, LATE))

    left_side = lax.broadcasted_iota(jnp.int32, (R, 128), 1) < 64

    def shard_of(d1, d2):
        rows = pl.ds(pl.multiple_of(slot_of(d1, d2) * H, 32), H)
        half = half_of(d1, d2)
        main = ip[rows, pl.ds(pl.multiple_of(half * 512, 512), 512)]
        low, high = ip[rows, pl.ds(1024, 128)][:R], ip[rows, pl.ds(1024, 128)][R:]
        rest = jnp.where(
            half == 0,
            jnp.where(left_side, low, pltpu.roll(high, 64, 1)),
            jnp.where(left_side, pltpu.roll(low, 64, 1), high),
        )
        return main, rest

    def send_shard(kind, key, place, shard, mains, rests_out, mains_in, rests_in, to):
        rows = pl.ds(place * H, H)
        mains[rows, :] = shard[0].astype(BF16)
        copy_of(kind, key, mains.at[rows, :], mains_in.at[rows, :], to).start()
        rows = blocks(place)
        rests_out[rows, :] = shard[1].astype(BF16)
        copy_of(kind, key, rests_out.at[rows, :], rests_in.at[rows, :], to).start()

    def add_shard(shard, place, mains_in, rests_in):
        return (
            shard[0] + mains_in[pl.ds(place * H, H), :].astype(F32),
            shard[1] + rests_in[blocks(place), :].astype(F32),
        )

    def send_b(d1, d2):
        to = {1: "bp", 2: "b2", 3: "bm"}[d2]
        shard = shard_of(d1, d2)
        send_shard("bo", ("bo", d1), 4 * d2 + d1, shard, b_main, b_rest, b_main_in, b_rest_in, to)

    def raw_inner(slot, carry):
        rows = pl.ds(pl.multiple_of(slot * H, 32), H)
        total = jnp.concatenate(rests(slot), axis=0) * ip[rows, pl.ds(1024, 128)]
        for q in range(4):
            product = rmain[q, rows, :].astype(F32) * ip[rows, pl.ds(256 * q, 256)]
            total = total + product[:, :128] + product[:, 128:]
        high = total.astype(BF16)
        low = (total - high.astype(F32)).astype(BF16)
        rows = pl.ds(pl.multiple_of(slot * 128, 128), H)
        inner_sums[rows, pl.ds(0, 128)] = high
        inner_sums[rows, pl.ds(128, 128)] = low
        return carry

    for d1 in range(4):
        for d2 in (1, 3):
            if d1 not in FORWARD or d2 != (1 if d1 in VIA_P else 3):
                got_i(("i", d1, d2))
    first, second, third = pl.ds(0, 4 * H), pl.ds(4 * H, 2 * H), pl.ds(6 * H, 2 * H)
    normalised(0, 4)
    got("s early", tbuf.at[blocks(0, 5), :])
    coef_of(0, 4, early)
    ip[first, :] = image_sums(0, 4, early)
    late_t(3)
    late_t(5)
    for d1 in (0, 1):
        got_i(("i", d1, 2))
    normalised(4, 2)
    coef_of(4, 2, early)
    late_t(4)
    tp[early[1], :] = text_sums(0, 6, early)
    ip[second, :] = image_sums(4, 2, early)

    got("s late", tbuf.at[blocks(0, 3), :])
    coef_of(0, 4, late)
    ip[first, :] += image_sums(0, 4, late)
    for d1 in (2, 1, 3, 0):
        for d2 in (1, 3):
            send_b(d1, d2)
    coef_of(4, 2, late)
    for d1 in (2, 3):
        got_i(("i", d1, 2))
    normalised(6, 2)
    coef_of(6, 2, late)
    coef_of(6, 2, early)

    def send_so(k):
        rows = blocks(k)
        sib_out[rows, :] = tp[blocks(OTHER[k]), :].astype(BF16)
        copy_of("so", ("so", k), sib_out.at[rows, :], sib_in.at[rows, :], "sib").start()

    tp[late[1], :] = text_sums(0, 8, late)
    for k in (4, 5, 3):
        send_so(k)
    tp[early[1], :] += text_sums(6, 2, early)
    for k in (6, 2, 7, 1, 0):
        send_so(k)
    def z_pass(k, to, new):
        got(("so", k), sib_in.at[blocks(k), :])
        for p in pieces:
            rows = rows_of(k, p)
            total = tp[rows_of(OWN[k], p), :] + sib_in[rows, :].astype(F32)
            for came in (k,) if k not in (4, 5) else ():
                place = rows_of(came, p)
                got(("zo", came, p), z_in.at[place, :])
                total = total + z_in[place, :].astype(F32)
            z_out[rows, :] = total.astype(BF16)
            key = ("zo", new) if new in (0, 8) else ("zo", new, p)
            slot = 4 if new == 8 else new
            copy_of("zo", key, z_out.at[rows, :], z_in.at[rows_of(slot, p), :], to).start()

    z_pass(4, "zp", 3)
    z_pass(5, "zm", 6)
    ip[second, :] += image_sums(4, 2, late)
    ip[third, :] = image_sums(6, 2, early) + image_sums(6, 2, late)
    for d1 in (2, 1, 3, 0):
        send_b(d1, 2)

    def b_sum(d1):
        got(("bo", d1), tbuf.at[blocks(0, 3), :])
        shard = shard_of(d1, 0)
        for d2 in (1, 2, 3):
            shard = add_shard(shard, 4 * d2 + d1, b_main_in, b_rest_in)
        return shard

    def send_a(d1, to):
        send_shard("ao", "ao", d1, b_sum(d1), a_main, a_rest, a_main_in, a_rest_in, to)

    def inner_b():
        lax.fori_loop(0, 8, raw_inner, 0)
        along = lax.dot_general(
            jnp.ones((8, 256), BF16), inner_sums[...], (((1,), (1,)), ((), ())), preferred_element_type=F32
        )
        for slot in range(8):
            inner_slots[slot] = along[:, slot * 128:(slot + 1) * 128]
        for d2 in (1, 2, 3):
            for d1 in range(4):
                b_inner[4 * d2 + d1] = inner_slots[slot_of(d1, d2)]
            four = pl.ds(4 * d2, 4)
            to = {1: "bp", 2: "b2", 3: "bm"}[d2]
            copy_of("bi", "bi", b_inner.at[four], b_inner_in.at[four], to).start()

    def inner_sum(d1):
        return inner_slots[slot_of(d1, 0)] + b_inner_in[4 + d1] + b_inner_in[8 + d1] + b_inner_in[12 + d1]

    def inner_a():
        got("bi", b_inner.at[pl.ds(4, 12)])
        for d1, to in ((1, "ap"), (2, "a2"), (3, "am")):
            a_inner[d1] = inner_sum(d1)
            copy_of("ai", "ai", a_inner.at[d1], a_inner_in.at[d1], to).start()

    z_pass(3, "zp", 2)
    z_pass(6, "zm", 7)
    inner_b()
    send_a(2, "a2")
    z_pass(2, "zp", 1)
    z_pass(7, "zm", 8)
    send_a(1, "ap")
    send_a(3, "am")
    inner_a()
    z_pass(1, "zp", 0)

    def back_norm(unit_rows, scale, inner, direction):
        return scale * (direction - unit_rows * inner)

    own_rows = pl.ds(4 * H, H)
    squares = jnp.concatenate(rests(4), axis=0) ** 2
    for q in range(4):
        part = rmain[q, own_rows, :].astype(F32)
        squares = squares + part[:, :128] ** 2 + part[:, 128:] ** 2
    scale_i = lax.rsqrt(jnp.sum(squares, axis=-1, keepdims=True) + 1e-06)
    unit_main = jnp.concatenate([rmain[2 * xh + i, own_rows, :].astype(F32) for i in (0, 1)], axis=1) * scale_i
    scale_rest = jnp.where(left_side, scale_i[:R], scale_i[R:])
    unit_rest = rrem[xh, blocks(4), :].astype(F32) * scale_rest
    got("ai", a_inner.at[pl.ds(1, 3)])
    along = inner_sum(0) + a_inner_in[1] + a_inner_in[2] + a_inner_in[3]
    inner_i = scale_i * jnp.transpose(jnp.broadcast_to(along[:1], (128, 128)))[:H, :1]
    inner_rest = jnp.where(left_side, inner_i[:R], inner_i[R:])

    got(("so", 0), sib_in.at[blocks(0), :])
    got(("zo", 0), z_in.at[blocks(0), :])
    got(("zo", 8), z_in.at[blocks(4), :])
    direction = tp[blocks(0), :] + sib_in[blocks(0), :].astype(F32)
    direction = direction + z_in[blocks(0), :].astype(F32) + z_in[blocks(4), :].astype(F32)
    text_unit, text_scale = tunit[...], tscales[:, :1]
    text_inner = jnp.sum(text_unit * direction, axis=-1, keepdims=True)
    text_grad = back_norm(text_unit, text_scale, text_inner, direction)
    otxt[...] = jnp.concatenate([quarter(text_grad, j) for j in range(4)], axis=1).astype(BF16)

    shard = b_sum(0)
    got("ao", tbuf.at[blocks(0, 3), :])
    for d1 in (1, 2, 3):
        shard = add_shard(shard, d1, a_main_in, a_rest_in)
    grad = back_norm(unit_main, scale_i, inner_i, shard[0]).astype(BF16)
    g_main[0] = grad[:, :256]
    g_main[1] = grad[:, 256:]
    g_rest[...] = back_norm(unit_rest, scale_rest, inner_rest, shard[1]).astype(BF16)
    copy_of("g", "g", g_main.at[1 - c], g_main_in, "sib").start()
    copy_of("h", "g", g_rest, g_rest_in, "sib").start()

    def put_image(rows, main, rest):
        rest = rest.astype(F32)
        low = jnp.where(c == 0, rest[:, :32], rest[:, 32:64])
        high = jnp.where(c == 0, rest[:, 64:96], rest[:, 96:])
        oimg[rows, pl.ds(0, 256)] = main
        oimg[rows, pl.ds(256, 32)] = jnp.concatenate([low, high], axis=0).astype(BF16)

    put_image(here, g_main[c], g_rest[...])

    left("x", rmain.at[0, pl.ds(0, H), :])
    left("y", xrem)
    left("t", tbuf.at[blocks(0, 7), :])
    left("s", tbuf.at[blocks(0, 8), :])
    left("i", ibuf.at[blocks(0, 15), :])
    left("so", sib_out)
    left("bo", tbuf.at[blocks(0, 12), :])
    left("zo", z_out.at[blocks(0, 7), :])
    left("ao", tbuf.at[blocks(0, 3), :])
    left("bi", b_inner.at[pl.ds(4, 12)])
    left("ai", a_inner.at[pl.ds(1, 3)])
    got("g", rrem.at[0, pl.ds(0, 5 * R), :])
    put_image(there, g_main_in[...], g_rest_in[...])
    left("g", g_main.at[0])
    left("h", g_rest)
    assert (len(send_ids), len(recv_ids)) == (SENDS, RECVS), (len(send_ids), len(recv_ids))


def on_device(image_features, text_features):
    vmem = pltpu.VMEM
    return pl.pallas_call(
        kernel,
        out_shape=(
            jax.ShapeDtypeStruct((4 * R, Q), BF16),
            jax.ShapeDtypeStruct((R, D), BF16),
        ),
        in_specs=[pl.BlockSpec(memory_space=pl.ANY)] * 2,
        out_specs=(pl.BlockSpec(memory_space=vmem), pl.BlockSpec(memory_space=vmem)),
        scratch_shapes=[
            vmem((4 * R, Q), BF16),
            vmem((R, 128), BF16),
            vmem((R, 128), BF16),
            vmem((4, N, 256), BF16),
            vmem((2, N // 2, 128), BF16),
            vmem((R, D), BF16),
            vmem((R, D), F32),
            vmem((R, 128), F32),
            vmem((N, D), BF16),
            vmem((N, D), BF16),
            vmem((N, EARLY), BF16),
            vmem((N, LATE), BF16),
            vmem((N, D), F32),
            vmem((N, D), F32),
            vmem((8 * R, D), BF16),
            vmem((8 * R, D), BF16),
            vmem((8 * R, D), BF16),
            vmem((8 * R, D), BF16),
            vmem((16 * H, 512), BF16),
            vmem((16 * R, 128), BF16),
            vmem((16 * H, 512), BF16),
            vmem((16 * R, 128), BF16),
            vmem((4 * H, 512), BF16),
            vmem((4 * R, 128), BF16),
            vmem((4 * H, 512), BF16),
            vmem((4 * R, 128), BF16),
            vmem((8 * 128, 256), BF16),
            vmem((8, 8, 128), F32),
            vmem((16, 8, 128), F32),
            vmem((16, 8, 128), F32),
            vmem((4, 8, 128), F32),
            vmem((4, 8, 128), F32),
            vmem((2, H, 256), BF16),
            vmem((R, 128), BF16),
            vmem((H, 256), BF16),
            vmem((R, 128), BF16),
            pltpu.SemaphoreType.DMA((SENDS,)),
            pltpu.SemaphoreType.DMA((RECVS,)),
            pltpu.SemaphoreType.DMA((3,)),
        ],
        compiler_params=pltpu.CompilerParams(
            collective_id=0, has_side_effects=True, vmem_limit_bytes=60 * 1024 * 1024
        ),
        cost_estimate=pl.CostEstimate(
            flops=6 * N * N * D, bytes_accessed=8 * R * D, transcendentals=N * N
        ),
    )(image_features, text_features)


def solution(mesh):
    placed = (P("loop", "grp"), P(("loop", "grp"), None))
    return jax.shard_map(
        on_device, mesh=mesh, in_specs=placed, out_specs=placed, check_vma=False
    )
```

```python
import jax
import jax.numpy as jnp
from jax import lax
from jax.experimental import pallas as pl
from jax.experimental.pallas import tpu as pltpu
from jax.sharding import PartitionSpec as P

LOGIT_SCALE = 16.0
LOGIT_BIAS = -4.0
BF16 = jnp.bfloat16
F32 = jnp.float32
H = 96
R = 48
D = 1152
Q = 288
N = 768
PIECES = 3
PR = R // PIECES
SENDS = 13
RECVS = 66
GREETED = ("zp", "zm", "zp2", "zm2", "ap", "am", "bp", "bm", "x2", "y2", "sib")
MESH = pl.DeviceIdType.MESH
FORWARD = (0, 1, 3, 2)
OWN = {0: 0, 1: 1, 7: 2, 2: 3, 6: 4, 3: 10, 5: 11, 4: 12}
OTHER = {k: place + (5 if place < 5 else 3) for k, place in OWN.items()}
EARLY = 10 * R
LATE = N - EARLY
VIA_P = (0, 2)


def neighbours():
    loop = lax.axis_index("loop")
    grp = lax.axis_index("grp")
    z = loop // 8
    x = (grp // 2) * 2 + (loop // 4) % 2
    y = loop % 4
    c = grp % 2

    def dev(dz, dx, dy, flip=0):
        zz = (z + dz + 8) % 8
        xx = (x + dx + 4) % 4
        yy = (y + dy + 4) % 4
        return (zz * 8 + (xx % 2) * 4 + yy, (xx // 2) * 2 + (c + flip) % 2)

    f = 1 - 2 * c
    return {
        "zp": dev(f, 0, 0),
        "zm": dev(-f, 0, 0),
        "zp2": dev(2 * f, 0, 0),
        "zm2": dev(-2 * f, 0, 0),
        "ap": dev(0, 1 - c, c),
        "am": dev(0, c - 1, -c),
        "bp": dev(0, c, 1 - c),
        "bm": dev(0, -c, c - 1),
        "a2": dev(0, 2 - 2 * c, 2 * c),
        "b2": dev(0, 2 * c, 2 - 2 * c),
        "x2": dev(0, 2, 0),
        "y2": dev(0, 0, 2),
        "sib": dev(0, 0, 0, 1),
    }, grp, x, c


def unit_of(values):
    scale = lax.rsqrt(jnp.sum(values * values, axis=-1, keepdims=True) + 1e-06)
    return values * scale, scale


def permuted(values):
    mains = [values[:, q * Q:q * Q + 256] for q in range(4)]
    return jnp.concatenate(mains + [values[:, q * Q + 256:(q + 1) * Q] for q in range(4)], axis=1)


def quarter(values, q):
    return jnp.concatenate(
        [values[:, q * 256:(q + 1) * 256], values[:, 1024 + q * 32:1024 + (q + 1) * 32]], axis=1
    )


def kernel(
    img, txt, oimg, otxt,
    ximg, xrem, srem, rmain, rrem, tin, tunit, tscales, ibuf, tbuf, coef_early, coef_late, ip, tp,
    sib_out, sib_in, z_out, z_in, b_main, b_rest, b_main_in, b_rest_in, a_main, a_rest, a_main_in, a_rest_in,
    inner_sums, inner_slots, b_inner, b_inner_in, a_inner, a_inner_in, g_main, g_rest, g_main_in, g_rest_in,
    send_sems, recv_sems, local_sems,
):
    dev, grp, x, c = neighbours()
    xh = x // 2
    send_ids = {}
    recv_ids = {}

    def copy_of(kind, key, src, dst, to):
        out = send_ids.setdefault(kind, len(send_ids))
        arrive = recv_ids.setdefault(key, len(recv_ids))
        return pltpu.make_async_remote_copy(
            src_ref=src, dst_ref=dst, send_sem=send_sems.at[out],
            recv_sem=recv_sems.at[arrive], device_id=dev[to], device_id_type=MESH,
        )

    def got(key, ref):
        pltpu.make_async_copy(ref, ref, recv_sems.at[recv_ids[key]]).wait()

    def left(kind, ref):
        pltpu.make_async_copy(ref, ref, send_sems.at[send_ids[kind]]).wait()

    def blocks(slot, count=1):
        return pl.ds(slot * R, count * R)

    def rows_of(slot, piece):
        return pl.ds(slot * R + piece * PR, PR)

    pieces = range(PIECES)
    load_t = pltpu.make_async_copy(txt, tin, local_sems.at[0])
    load_t.start()
    load_i = pltpu.make_async_copy(img, ximg, local_sems.at[1])
    load_i.start()

    barrier = pltpu.get_barrier_semaphore()
    for name in GREETED:
        pl.semaphore_signal(barrier, inc=1, device_id=dev[name], device_id_type=MESH)
    load_t.wait()
    unit, tscale = unit_of(permuted(tin[...].astype(F32)))
    tbuf[blocks(0), :] = unit.astype(BF16)
    tunit[...] = unit
    tscales[...] = jnp.broadcast_to(tscale, (R, 128))
    inner_sums[...] = jnp.zeros_like(inner_sums)
    load_i.wait()

    def rest_of(half):
        rest = ximg[pl.ds(pl.multiple_of(half * H, 32), H), 256:].astype(F32)
        low, high = rest[:R], rest[R:]
        gap = jnp.zeros_like(low)
        return jnp.where(
            c == 0,
            jnp.concatenate([low, gap, high, gap], axis=1),
            jnp.concatenate([gap, low, gap, high], axis=1),
        )

    xrem[...] = rest_of(1 - c).astype(BF16)
    rest_here = rest_of(c)
    there = pl.ds(pl.multiple_of((1 - c) * H, 32), H)
    here = pl.ds(pl.multiple_of(c * H, 32), H)
    rmain[grp, pl.ds(4 * H, H), :] = ximg[here, :256]
    pl.semaphore_wait(barrier, len(GREETED))

    copy_of("x", "x", ximg.at[there, pl.ds(0, 256)], rmain.at[grp, pl.ds(4 * H, H), :], "sib").start()
    copy_of("y", "x", xrem, srem, "sib").start()

    def send_t(to, slot, new, piece):
        key = ("t", new) if new in (3, 4, 5) else ("t", new, piece)
        src, dst = rows_of(OWN[slot], piece), rows_of(OWN[new], piece)
        copy_of("t", key, tbuf.at[src, :], tbuf.at[dst, :], to).start()

    def send_s(slot):
        key = "s late" if slot in (3, 5, 4) else "s early"
        src, dst = blocks(OWN[slot]), blocks(OTHER[slot])
        copy_of("s", key, tbuf.at[src, :], tbuf.at[dst, :], "sib").start()

    for p in pieces:
        send_t("zm", 0, 1, p)
        send_t("zp", 0, 7, p)
    send_s(0)

    def slot_of(d1, d2):
        return 4 * (1 - d2 % 2) + (1 - c) * ((d2 // 2) * 2 + d1 % 2) + c * d1

    def half_of(d1, d2):
        return ((x + (1 - c) * d1 + c * d2) % 4) // 2

    def send_i(to, source, target, key):
        half = half_of(*source)
        quarters = pl.ds(2 * half, 2)
        came, goes = slot_of(*source), slot_of(*target)
        src = pl.ds(pl.multiple_of(came * H, 32), H)
        dst = pl.ds(pl.multiple_of(goes * H, 32), H)
        copy_of("i", key, rmain.at[quarters, src, :], rmain.at[quarters, dst, :], to).start()
        src = pl.ds(pl.multiple_of(came * R, 16), R)
        dst = pl.ds(pl.multiple_of(goes * R, 16), R)
        copy_of("i", key, rrem.at[half, src, :], rrem.at[half, dst, :], to).start()

    def got_i(key):
        got(key, tbuf.at[blocks(0), :])

    def near_b(d1):
        send_i("bm", (d1, 0), (d1, 1), ("i", d1, 1))
        send_i("bp", (d1, 0), (d1, 3), ("i", d1, 3))
        if d1 not in FORWARD:
            send_i("b2", (d1, 0), (d1, 2), ("i", d1, 2))

    def far_b(d1):
        if d1 in VIA_P:
            got_i(("i", d1, 1))
            send_i("bm", (d1, 1), (d1, 2), ("i", d1, 2))
        else:
            got_i(("i", d1, 3))
            send_i("bp", (d1, 3), (d1, 2), ("i", d1, 2))

    got("x", rrem.at[0, pl.ds(0, 5 * R), :])
    rrem[xh, pl.ds(4 * R, R), :] = (rest_here + srem[...].astype(F32)).astype(BF16)
    send_i("am", (0, 0), (1, 0), ("i", 1, 0))
    send_i("ap", (0, 0), (3, 0), ("i", 3, 0))
    send_i("a2", (0, 0), (2, 0), ("i", 2, 0))
    near_b(0)

    def ring_t(new_m, new_p):
        for p in pieces:
            got(("t", new_m, p), tbuf.at[rows_of(OWN[new_m], p), :])
            send_t("zm", new_m, new_m + 1, p)
            if new_p == 6:
                send_t("zm2", 2, 4, p)
            got(("t", new_p, p), tbuf.at[rows_of(OWN[new_p], p), :])
            send_t("zp", new_p, new_p - 1, p)
        send_s(new_m)
        send_s(new_p)

    ring_t(1, 7)
    for d1 in (1, 3):
        got_i(("i", d1, 0))
        near_b(d1)
    got_i(("i", 2, 0))
    near_b(2)
    ring_t(2, 6)
    for d1 in FORWARD:
        far_b(d1)

    def late_t(slot):
        got(("t", slot), tbuf.at[blocks(OWN[slot]), :])
        send_s(slot)

    def rests(slot):
        rows = pl.ds(pl.multiple_of(slot * R, 16), R)
        first, second = rrem[0, rows, :].astype(F32), rrem[1, rows, :].astype(F32)
        left_side = lax.broadcasted_iota(jnp.int32, first.shape, 1) < 64
        low = jnp.where(left_side, first, pltpu.roll(second, 64, 1))
        high = jnp.where(left_side, pltpu.roll(first, 64, 1), second)
        return low, high

    def normalise(slot, carry):
        rows = pl.ds(pl.multiple_of(slot * H, 32), H)
        parts = [rmain[q, rows, :].astype(F32) for q in range(4)]
        parts.append(jnp.concatenate(rests(slot), axis=0))
        squares = [jnp.sum(part * part, axis=-1, keepdims=True) for part in parts]
        scale = lax.rsqrt(sum(squares[1:], squares[0]) + 1e-06)
        for q, part in enumerate(parts):
            ibuf[rows, pl.ds(256 * q, part.shape[1])] = (part * scale).astype(BF16)
        return carry

    def normalised(slot, count):
        lax.fori_loop(slot, slot + count, normalise, 0)

    def coef_of(slot, count, part):
        store, texts = part
        rows = pl.ds(slot * H, count * H)
        logits = LOGIT_SCALE * lax.dot_general(
            ibuf[rows, :], tbuf[texts, :], (((1,), (1,)), ((), ())), preferred_element_type=F32
        ) + LOGIT_BIAS
        chance = jax.nn.sigmoid(logits)
        if slot == 4 and part is early:
            row_ids = lax.broadcasted_iota(jnp.int32, chance.shape, 0)
            col_ids = lax.broadcasted_iota(jnp.int32, chance.shape, 1)
            start = OTHER[0] * R
            own = (col_ids < R) & (row_ids == col_ids + c * R)
            other = (col_ids >= start) & (col_ids < start + R) & (row_ids == col_ids - start + (1 - c) * R)
            chance = chance - jnp.where((own | other) & (c == xh), 1.0, 0.0)
        store[rows, :] = (LOGIT_SCALE * chance).astype(BF16)

    def image_sums(slot, count, part):
        store, texts = part
        rows = pl.ds(slot * H, count * H)
        return jnp.dot(store[rows, :], tbuf[texts, :], preferred_element_type=F32)

    def text_sums(slot, count, part):
        rows = pl.ds(slot * H, count * H)
        return lax.dot_general(
            part[0][rows, :], ibuf[rows, :], (((0,), (0,)), ((), ())), preferred_element_type=F32
        )

    early = (coef_early, pl.ds(0, EARLY))
    late = (coef_late, pl.ds(EARLY, LATE))

    left_side = lax.broadcasted_iota(jnp.int32, (R, 128), 1) < 64

    def shard_of(d1, d2):
        rows = pl.ds(pl.multiple_of(slot_of(d1, d2) * H, 32), H)
        half = half_of(d1, d2)
        main = ip[rows, pl.ds(pl.multiple_of(half * 512, 512), 512)]
        low, high = ip[rows, pl.ds(1024, 128)][:R], ip[rows, pl.ds(1024, 128)][R:]
        rest = jnp.where(
            half == 0,
            jnp.where(left_side, low, pltpu.roll(high, 64, 1)),
            jnp.where(left_side, pltpu.roll(low, 64, 1), high),
        )
        return main, rest

    def send_shard(kind, key, place, shard, mains, rests_out, mains_in, rests_in, to):
        rows = pl.ds(place * H, H)
        mains[rows, :] = shard[0].astype(BF16)
        copy_of(kind, key, mains.at[rows, :], mains_in.at[rows, :], to).start()
        rows = blocks(place)
        rests_out[rows, :] = shard[1].astype(BF16)
        copy_of(kind, key, rests_out.at[rows, :], rests_in.at[rows, :], to).start()

    def add_shard(shard, place, mains_in, rests_in):
        return (
            shard[0] + mains_in[pl.ds(place * H, H), :].astype(F32),
            shard[1] + rests_in[blocks(place), :].astype(F32),
        )

    def send_b(d1, d2):
        to = {1: "bp", 2: "b2", 3: "bm"}[d2]
        shard = shard_of(d1, d2)
        send_shard("bo", ("bo", d1), 4 * d2 + d1, shard, b_main, b_rest, b_main_in, b_rest_in, to)

    def raw_inner(slot, carry):
        rows = pl.ds(pl.multiple_of(slot * H, 32), H)
        total = jnp.concatenate(rests(slot), axis=0) * ip[rows, pl.ds(1024, 128)]
        for q in range(4):
            product = rmain[q, rows, :].astype(F32) * ip[rows, pl.ds(256 * q, 256)]
            total = total + product[:, :128] + product[:, 128:]
        high = total.astype(BF16)
        low = (total - high.astype(F32)).astype(BF16)
        rows = pl.ds(pl.multiple_of(slot * 128, 128), H)
        inner_sums[rows, pl.ds(0, 128)] = high
        inner_sums[rows, pl.ds(128, 128)] = low
        return carry

    for d1 in range(4):
        for d2 in (1, 3):
            if d1 not in FORWARD or d2 != (1 if d1 in VIA_P else 3):
                got_i(("i", d1, d2))
    first, second, third = pl.ds(0, 4 * H), pl.ds(4 * H, 2 * H), pl.ds(6 * H, 2 * H)
    normalised(0, 4)
    got("s early", tbuf.at[blocks(0, 5), :])
    coef_of(0, 4, early)
    ip[first, :] = image_sums(0, 4, early)
    late_t(3)
    late_t(5)
    for d1 in (0, 1):
        got_i(("i", d1, 2))
    normalised(4, 2)
    coef_of(4, 2, early)
    late_t(4)
    tp[early[1], :] = text_sums(0, 6, early)
    ip[second, :] = image_sums(4, 2, early)

    got("s late", tbuf.at[blocks(0, 3), :])
    coef_of(0, 4, late)
    ip[first, :] += image_sums(0, 4, late)
    for d1 in (2, 1, 3, 0):
        for d2 in (1, 3):
            send_b(d1, d2)
    coef_of(4, 2, late)
    for d1 in (2, 3):
        got_i(("i", d1, 2))
    normalised(6, 2)
    coef_of(6, 2, late)
    coef_of(6, 2, early)

    def inner_b():
        lax.fori_loop(0, 8, raw_inner, 0)
        along = lax.dot_general(
            jnp.ones((8, 256), BF16), inner_sums[...], (((1,), (1,)), ((), ())), preferred_element_type=F32
        )
        for slot in range(8):
            inner_slots[slot] = along[:, slot * 128:(slot + 1) * 128]
        for d2 in (1, 2, 3):
            for d1 in range(4):
                b_inner[4 * d2 + d1] = inner_slots[slot_of(d1, d2)]
            four = pl.ds(4 * d2, 4)
            to = {1: "bp", 2: "b2", 3: "bm"}[d2]
            copy_of("bi", "bi", b_inner.at[four], b_inner_in.at[four], to).start()

    def send_so(k):
        rows = blocks(k)
        sib_out[rows, :] = tp[blocks(OTHER[k]), :].astype(BF16)
        copy_of("so", ("so", k), sib_out.at[rows, :], sib_in.at[rows, :], "sib").start()

    tp[late[1], :] = text_sums(0, 8, late)
    for k in (4, 5, 3):
        send_so(k)
    tp[early[1], :] += text_sums(6, 2, early)
    for k in (6, 2, 7, 1, 0):
        send_so(k)
    def z_pass(*hops):
        for k, to, new in hops:
            got(("so", k), sib_in.at[blocks(k), :])
        for p in pieces:
            for k, to, new in hops:
                rows = rows_of(k, p)
                total = tp[rows_of(OWN[k], p), :] + sib_in[rows, :].astype(F32)
                if k not in (4, 5):
                    got(("zo", k, p), z_in.at[rows, :])
                    total = total + z_in[rows, :].astype(F32)
                z_out[rows, :] = total.astype(BF16)
                key = ("zo", new) if new in (0, 8) else ("zo", new, p)
                slot = 4 if new == 8 else new
                copy_of("zo", key, z_out.at[rows, :], z_in.at[rows_of(slot, p), :], to).start()

    z_pass((4, "zp", 3), (5, "zm", 6))
    ip[second, :] += image_sums(4, 2, late)
    ip[third, :] = image_sums(6, 2, early) + image_sums(6, 2, late)
    inner_b()
    for d1 in (2, 1, 3, 0):
        send_b(d1, 2)

    def b_sum(d1):
        got(("bo", d1), tbuf.at[blocks(0, 3), :])
        shard = shard_of(d1, 0)
        for d2 in (1, 2, 3):
            shard = add_shard(shard, 4 * d2 + d1, b_main_in, b_rest_in)
        return shard

    def send_a(d1, to):
        send_shard("ao", "ao", d1, b_sum(d1), a_main, a_rest, a_main_in, a_rest_in, to)

    def inner_sum(d1):
        return inner_slots[slot_of(d1, 0)] + b_inner_in[4 + d1] + b_inner_in[8 + d1] + b_inner_in[12 + d1]

    def inner_a():
        got("bi", b_inner.at[pl.ds(4, 12)])
        for d1, to in ((1, "ap"), (2, "a2"), (3, "am")):
            a_inner[d1] = inner_sum(d1)
            copy_of("ai", "ai", a_inner.at[d1], a_inner_in.at[d1], to).start()

    z_pass((3, "zp", 2), (6, "zm", 7))
    send_a(2, "a2")
    z_pass((2, "zp", 1), (7, "zm", 8))
    send_a(1, "ap")
    send_a(3, "am")
    inner_a()
    z_pass((1, "zp", 0))

    def back_norm(unit_rows, scale, inner, direction):
        return scale * (direction - unit_rows * inner)

    own_rows = pl.ds(4 * H, H)
    squares = jnp.concatenate(rests(4), axis=0) ** 2
    for q in range(4):
        part = rmain[q, own_rows, :].astype(F32)
        squares = squares + part[:, :128] ** 2 + part[:, 128:] ** 2
    scale_i = lax.rsqrt(jnp.sum(squares, axis=-1, keepdims=True) + 1e-06)
    unit_main = jnp.concatenate([rmain[2 * xh + i, own_rows, :].astype(F32) for i in (0, 1)], axis=1) * scale_i
    scale_rest = jnp.where(left_side, scale_i[:R], scale_i[R:])
    unit_rest = rrem[xh, blocks(4), :].astype(F32) * scale_rest
    got("ai", a_inner.at[pl.ds(1, 3)])
    along = inner_sum(0) + a_inner_in[1] + a_inner_in[2] + a_inner_in[3]
    inner_i = scale_i * jnp.transpose(jnp.broadcast_to(along[:1], (128, 128)))[:H, :1]
    inner_rest = jnp.where(left_side, inner_i[:R], inner_i[R:])

    shard = b_sum(0)
    got("ao", tbuf.at[blocks(0, 3), :])
    for d1 in (1, 2, 3):
        shard = add_shard(shard, d1, a_main_in, a_rest_in)
    grad = back_norm(unit_main, scale_i, inner_i, shard[0]).astype(BF16)
    g_main[0] = grad[:, :256]
    g_main[1] = grad[:, 256:]
    g_rest[...] = back_norm(unit_rest, scale_rest, inner_rest, shard[1]).astype(BF16)
    copy_of("g", "g", g_main.at[1 - c], g_main_in, "sib").start()
    copy_of("h", "g", g_rest, g_rest_in, "sib").start()

    def put_image(rows, main, rest):
        rest = rest.astype(F32)
        low = jnp.where(c == 0, rest[:, :32], rest[:, 32:64])
        high = jnp.where(c == 0, rest[:, 64:96], rest[:, 96:])
        oimg[rows, pl.ds(0, 256)] = main
        oimg[rows, pl.ds(256, 32)] = jnp.concatenate([low, high], axis=0).astype(BF16)

    put_image(here, g_main[c], g_rest[...])

    got(("so", 0), sib_in.at[blocks(0), :])
    got(("zo", 0), z_in.at[blocks(0), :])
    got(("zo", 8), z_in.at[blocks(4), :])
    direction = tp[blocks(0), :] + sib_in[blocks(0), :].astype(F32)
    direction = direction + z_in[blocks(0), :].astype(F32) + z_in[blocks(4), :].astype(F32)
    text_unit, text_scale = tunit[...], tscales[:, :1]
    text_inner = jnp.sum(text_unit * direction, axis=-1, keepdims=True)
    text_grad = back_norm(text_unit, text_scale, text_inner, direction)
    otxt[...] = jnp.concatenate([quarter(text_grad, j) for j in range(4)], axis=1).astype(BF16)

    left("x", rmain.at[0, pl.ds(0, H), :])
    left("y", xrem)
    left("t", tbuf.at[blocks(0, 7), :])
    left("s", tbuf.at[blocks(0, 8), :])
    left("i", ibuf.at[blocks(0, 15), :])
    left("so", sib_out)
    left("bo", tbuf.at[blocks(0, 12), :])
    left("zo", z_out.at[blocks(0, 7), :])
    left("ao", tbuf.at[blocks(0, 3), :])
    left("bi", b_inner.at[pl.ds(4, 12)])
    left("ai", a_inner.at[pl.ds(1, 3)])
    got("g", rrem.at[0, pl.ds(0, 5 * R), :])
    put_image(there, g_main_in[...], g_rest_in[...])
    left("g", g_main.at[0])
    left("h", g_rest)
    assert (len(send_ids), len(recv_ids)) == (SENDS, RECVS), (len(send_ids), len(recv_ids))


def hand_out(image_grad, text_grad, oimg, otxt, sems):
    copies = [
        pltpu.make_async_copy(image_grad, oimg, sems.at[0]),
        pltpu.make_async_copy(text_grad, otxt, sems.at[1]),
    ]
    for copy in copies:
        copy.start()
    for copy in copies:
        copy.wait()


def on_device(image_features, text_features):
    vmem = pltpu.VMEM
    image_grad, text_grad = pl.pallas_call(
        kernel,
        out_shape=(
            jax.ShapeDtypeStruct((4 * R, Q), BF16),
            jax.ShapeDtypeStruct((R, D), BF16),
        ),
        in_specs=[pl.BlockSpec(memory_space=pl.ANY)] * 2,
        out_specs=(pl.BlockSpec(memory_space=vmem), pl.BlockSpec(memory_space=vmem)),
        scratch_shapes=[
            vmem((4 * R, Q), BF16),
            vmem((R, 128), BF16),
            vmem((R, 128), BF16),
            vmem((4, N, 256), BF16),
            vmem((2, N // 2, 128), BF16),
            vmem((R, D), BF16),
            vmem((R, D), F32),
            vmem((R, 128), F32),
            vmem((N, D), BF16),
            vmem((N, D), BF16),
            vmem((N, EARLY), BF16),
            vmem((N, LATE), BF16),
            vmem((N, D), F32),
            vmem((N, D), F32),
            vmem((8 * R, D), BF16),
            vmem((8 * R, D), BF16),
            vmem((8 * R, D), BF16),
            vmem((8 * R, D), BF16),
            vmem((16 * H, 512), BF16),
            vmem((16 * R, 128), BF16),
            vmem((16 * H, 512), BF16),
            vmem((16 * R, 128), BF16),
            vmem((4 * H, 512), BF16),
            vmem((4 * R, 128), BF16),
            vmem((4 * H, 512), BF16),
            vmem((4 * R, 128), BF16),
            vmem((8 * 128, 256), BF16),
            vmem((8, 8, 128), F32),
            vmem((16, 8, 128), F32),
            vmem((16, 8, 128), F32),
            vmem((4, 8, 128), F32),
            vmem((4, 8, 128), F32),
            vmem((2, H, 256), BF16),
            vmem((R, 128), BF16),
            vmem((H, 256), BF16),
            vmem((R, 128), BF16),
            pltpu.SemaphoreType.DMA((SENDS,)),
            pltpu.SemaphoreType.DMA((RECVS,)),
            pltpu.SemaphoreType.DMA((3,)),
        ],
        compiler_params=pltpu.CompilerParams(
            collective_id=0, has_side_effects=True, vmem_limit_bytes=60 * 1024 * 1024
        ),
        cost_estimate=pl.CostEstimate(
            flops=6 * N * N * D, bytes_accessed=8 * R * D, transcendentals=N * N
        ),
    )(image_features, text_features)
    return pl.pallas_call(
        hand_out,
        out_shape=(
            jax.ShapeDtypeStruct((4 * R, Q), BF16),
            jax.ShapeDtypeStruct((R, D), BF16),
        ),
        in_specs=[pl.BlockSpec(memory_space=pltpu.VMEM)] * 2,
        out_specs=[pl.BlockSpec(memory_space=pltpu.HBM)] * 2,
        scratch_shapes=[pltpu.SemaphoreType.DMA((2,))],
    )(image_grad, text_grad)


def solution(mesh):
    placed = (P("loop", "grp"), P(("loop", "grp"), None))
    return jax.shard_map(
        on_device, mesh=mesh, in_specs=placed, out_specs=placed, check_vma=False
    )
```

```python
import jax
import jax.numpy as jnp
from jax import lax
from jax.experimental import pallas as pl
from jax.experimental.pallas import tpu as pltpu
from jax.sharding import PartitionSpec as P

LOGIT_SCALE = 16.0
LOGIT_BIAS = -4.0
BF16 = jnp.bfloat16
F32 = jnp.float32
H = 96
R = 48
D = 1152
Q = 288
N = 768
PIECES = 3
PR = R // PIECES
SENDS = 13
RECVS = 66
GREETED = ("zp", "zm", "zp2", "zm2", "ap", "am", "bp", "bm", "x2", "y2", "sib")
MESH = pl.DeviceIdType.MESH
FORWARD = (0, 1, 3, 2)
OWN = {0: 0, 1: 1, 7: 2, 2: 3, 6: 4, 3: 10, 5: 11, 4: 12}
OTHER = {k: place + (5 if place < 5 else 3) for k, place in OWN.items()}
EARLY = 10 * R
LATE = N - EARLY
VIA_P = (0, 2)


def neighbours():
    loop = lax.axis_index("loop")
    grp = lax.axis_index("grp")
    z = loop // 8
    x = (grp // 2) * 2 + (loop // 4) % 2
    y = loop % 4
    c = grp % 2

    def dev(dz, dx, dy, flip=0):
        zz = (z + dz + 8) % 8
        xx = (x + dx + 4) % 4
        yy = (y + dy + 4) % 4
        return (zz * 8 + (xx % 2) * 4 + yy, (xx // 2) * 2 + (c + flip) % 2)

    f = 1 - 2 * c
    return {
        "zp": dev(f, 0, 0),
        "zm": dev(-f, 0, 0),
        "zp2": dev(2 * f, 0, 0),
        "zm2": dev(-2 * f, 0, 0),
        "ap": dev(0, 1 - c, c),
        "am": dev(0, c - 1, -c),
        "bp": dev(0, c, 1 - c),
        "bm": dev(0, -c, c - 1),
        "a2": dev(0, 2 - 2 * c, 2 * c),
        "b2": dev(0, 2 * c, 2 - 2 * c),
        "x2": dev(0, 2, 0),
        "y2": dev(0, 0, 2),
        "sib": dev(0, 0, 0, 1),
    }, grp, x, c


def unit_of(values):
    scale = lax.rsqrt(jnp.sum(values * values, axis=-1, keepdims=True) + 1e-06)
    return values * scale, scale


def permuted(values):
    mains = [values[:, q * Q:q * Q + 256] for q in range(4)]
    return jnp.concatenate(mains + [values[:, q * Q + 256:(q + 1) * Q] for q in range(4)], axis=1)


def quarter(values, q):
    return jnp.concatenate(
        [values[:, q * 256:(q + 1) * 256], values[:, 1024 + q * 32:1024 + (q + 1) * 32]], axis=1
    )


def kernel(
    img, txt, oimg, otxt,
    ximg, xrem, srem, rmain, rrem, tin, tunit, tscales, ibuf, tbuf, coef_early, coef_late, ip, tp,
    sib_out, sib_in, z_out, z_in, b_main, b_rest, b_main_in, b_rest_in, a_main, a_rest, a_main_in, a_rest_in,
    inner_sums, inner_slots, b_inner, b_inner_in, a_inner, a_inner_in, g_main, g_rest, g_main_in, g_rest_in,
    send_sems, recv_sems, local_sems,
):
    dev, grp, x, c = neighbours()
    xh = x // 2
    send_ids = {}
    recv_ids = {}

    def copy_of(kind, key, src, dst, to):
        out = send_ids.setdefault(kind, len(send_ids))
        arrive = recv_ids.setdefault(key, len(recv_ids))
        return pltpu.make_async_remote_copy(
            src_ref=src, dst_ref=dst, send_sem=send_sems.at[out],
            recv_sem=recv_sems.at[arrive], device_id=dev[to], device_id_type=MESH,
        )

    def got(key, ref):
        pltpu.make_async_copy(ref, ref, recv_sems.at[recv_ids[key]]).wait()

    def left(kind, ref):
        pltpu.make_async_copy(ref, ref, send_sems.at[send_ids[kind]]).wait()

    def blocks(slot, count=1):
        return pl.ds(slot * R, count * R)

    def rows_of(slot, piece):
        return pl.ds(slot * R + piece * PR, PR)

    pieces = range(PIECES)
    load_t = pltpu.make_async_copy(txt, tin, local_sems.at[0])
    load_t.start()
    load_i = pltpu.make_async_copy(img, ximg, local_sems.at[1])
    load_i.start()

    barrier = pltpu.get_barrier_semaphore()
    for name in GREETED:
        pl.semaphore_signal(barrier, inc=1, device_id=dev[name], device_id_type=MESH)
    load_t.wait()
    unit, tscale = unit_of(permuted(tin[...].astype(F32)))
    tbuf[blocks(0), :] = unit.astype(BF16)
    tunit[...] = unit
    tscales[...] = jnp.broadcast_to(tscale, (R, 128))
    inner_sums[...] = jnp.zeros_like(inner_sums)
    load_i.wait()

    def rest_of(half):
        rest = ximg[pl.ds(pl.multiple_of(half * H, 32), H), 256:].astype(F32)
        low, high = rest[:R], rest[R:]
        gap = jnp.zeros_like(low)
        return jnp.where(
            c == 0,
            jnp.concatenate([low, gap, high, gap], axis=1),
            jnp.concatenate([gap, low, gap, high], axis=1),
        )

    xrem[...] = rest_of(1 - c).astype(BF16)
    rest_here = rest_of(c)
    there = pl.ds(pl.multiple_of((1 - c) * H, 32), H)
    here = pl.ds(pl.multiple_of(c * H, 32), H)
    rmain[grp, pl.ds(4 * H, H), :] = ximg[here, :256]
    pl.semaphore_wait(barrier, len(GREETED))

    def send_t(to, slot, new, piece):
        key = ("t", new) if new in (3, 4, 5) else ("t", new, piece)
        src, dst = rows_of(OWN[slot], piece), rows_of(OWN[new], piece)
        copy_of("t", key, tbuf.at[src, :], tbuf.at[dst, :], to).start()

    def send_s(slot):
        key = "s late" if slot in (3, 5, 4) else "s early"
        src, dst = blocks(OWN[slot]), blocks(OTHER[slot])
        copy_of("s", key, tbuf.at[src, :], tbuf.at[dst, :], "sib").start()

    for p in pieces:
        send_t("zm", 0, 1, p)
        send_t("zp", 0, 7, p)

    copy_of("x", "x", ximg.at[there, pl.ds(0, 256)], rmain.at[grp, pl.ds(4 * H, H), :], "sib").start()
    copy_of("y", "x", xrem, srem, "sib").start()
    send_s(0)

    def slot_of(d1, d2):
        return 4 * (1 - d2 % 2) + (1 - c) * ((d2 // 2) * 2 + d1 % 2) + c * d1

    def half_of(d1, d2):
        return ((x + (1 - c) * d1 + c * d2) % 4) // 2

    def send_i(to, source, target, key):
        half = half_of(*source)
        quarters = pl.ds(2 * half, 2)
        came, goes = slot_of(*source), slot_of(*target)
        src = pl.ds(pl.multiple_of(came * H, 32), H)
        dst = pl.ds(pl.multiple_of(goes * H, 32), H)
        copy_of("i", key, rmain.at[quarters, src, :], rmain.at[quarters, dst, :], to).start()
        src = pl.ds(pl.multiple_of(came * R, 16), R)
        dst = pl.ds(pl.multiple_of(goes * R, 16), R)
        copy_of("i", key, rrem.at[half, src, :], rrem.at[half, dst, :], to).start()

    def got_i(key):
        got(key, tbuf.at[blocks(0), :])

    def near_b(d1):
        send_i("bm", (d1, 0), (d1, 1), ("i", d1, 1))
        send_i("bp", (d1, 0), (d1, 3), ("i", d1, 3))
        if d1 not in FORWARD:
            send_i("b2", (d1, 0), (d1, 2), ("i", d1, 2))

    def far_b(d1):
        if d1 in VIA_P:
            got_i(("i", d1, 1))
            send_i("bm", (d1, 1), (d1, 2), ("i", d1, 2))
        else:
            got_i(("i", d1, 3))
            send_i("bp", (d1, 3), (d1, 2), ("i", d1, 2))

    got("x", rrem.at[0, pl.ds(0, 5 * R), :])
    rrem[xh, pl.ds(4 * R, R), :] = (rest_here + srem[...].astype(F32)).astype(BF16)
    send_i("am", (0, 0), (1, 0), ("i", 1, 0))
    send_i("ap", (0, 0), (3, 0), ("i", 3, 0))
    near_b(0)
    send_i("a2", (0, 0), (2, 0), ("i", 2, 0))

    def ring_t(new_m, new_p):
        for p in pieces:
            got(("t", new_m, p), tbuf.at[rows_of(OWN[new_m], p), :])
            send_t("zm", new_m, new_m + 1, p)
            if new_p == 6:
                send_t("zm2", 2, 4, p)
            got(("t", new_p, p), tbuf.at[rows_of(OWN[new_p], p), :])
            send_t("zp", new_p, new_p - 1, p)
        send_s(new_m)
        send_s(new_p)

    ring_t(1, 7)
    for d1 in (1, 3):
        got_i(("i", d1, 0))
        near_b(d1)
    got_i(("i", 2, 0))
    near_b(2)
    ring_t(2, 6)
    for d1 in FORWARD:
        far_b(d1)

    def late_t(slot):
        got(("t", slot), tbuf.at[blocks(OWN[slot]), :])
        send_s(slot)

    def rests(slot):
        rows = pl.ds(pl.multiple_of(slot * R, 16), R)
        first, second = rrem[0, rows, :].astype(F32), rrem[1, rows, :].astype(F32)
        left_side = lax.broadcasted_iota(jnp.int32, first.shape, 1) < 64
        low = jnp.where(left_side, first, pltpu.roll(second, 64, 1))
        high = jnp.where(left_side, pltpu.roll(first, 64, 1), second)
        return low, high

    def normalise(slot, carry):
        rows = pl.ds(pl.multiple_of(slot * H, 32), H)
        parts = [rmain[q, rows, :].astype(F32) for q in range(4)]
        parts.append(jnp.concatenate(rests(slot), axis=0))
        squares = [jnp.sum(part * part, axis=-1, keepdims=True) for part in parts]
        scale = lax.rsqrt(sum(squares[1:], squares[0]) + 1e-06)
        for q, part in enumerate(parts):
            ibuf[rows, pl.ds(256 * q, part.shape[1])] = (part * scale).astype(BF16)
        return carry

    def normalised(slot, count):
        lax.fori_loop(slot, slot + count, normalise, 0)

    def coef_of(slot, count, part):
        store, texts = part
        rows = pl.ds(slot * H, count * H)
        logits = LOGIT_SCALE * lax.dot_general(
            ibuf[rows, :], tbuf[texts, :], (((1,), (1,)), ((), ())), preferred_element_type=F32
        ) + LOGIT_BIAS
        chance = jax.nn.sigmoid(logits)
        if slot == 4 and part is early:
            row_ids = lax.broadcasted_iota(jnp.int32, chance.shape, 0)
            col_ids = lax.broadcasted_iota(jnp.int32, chance.shape, 1)
            start = OTHER[0] * R
            own = (col_ids < R) & (row_ids == col_ids + c * R)
            other = (col_ids >= start) & (col_ids < start + R) & (row_ids == col_ids - start + (1 - c) * R)
            chance = chance - jnp.where((own | other) & (c == xh), 1.0, 0.0)
        store[rows, :] = (LOGIT_SCALE * chance).astype(BF16)

    def image_sums(slot, count, part):
        store, texts = part
        rows = pl.ds(slot * H, count * H)
        return jnp.dot(store[rows, :], tbuf[texts, :], preferred_element_type=F32)

    def text_sums(slot, count, part):
        rows = pl.ds(slot * H, count * H)
        return lax.dot_general(
            part[0][rows, :], ibuf[rows, :], (((0,), (0,)), ((), ())), preferred_element_type=F32
        )

    early = (coef_early, pl.ds(0, EARLY))
    late = (coef_late, pl.ds(EARLY, LATE))

    left_side = lax.broadcasted_iota(jnp.int32, (R, 128), 1) < 64

    def shard_of(d1, d2):
        rows = pl.ds(pl.multiple_of(slot_of(d1, d2) * H, 32), H)
        half = half_of(d1, d2)
        main = ip[rows, pl.ds(pl.multiple_of(half * 512, 512), 512)]
        low, high = ip[rows, pl.ds(1024, 128)][:R], ip[rows, pl.ds(1024, 128)][R:]
        rest = jnp.where(
            half == 0,
            jnp.where(left_side, low, pltpu.roll(high, 64, 1)),
            jnp.where(left_side, pltpu.roll(low, 64, 1), high),
        )
        return main, rest

    def send_shard(kind, key, place, shard, mains, rests_out, mains_in, rests_in, to):
        rows = pl.ds(place * H, H)
        mains[rows, :] = shard[0].astype(BF16)
        copy_of(kind, key, mains.at[rows, :], mains_in.at[rows, :], to).start()
        rows = blocks(place)
        rests_out[rows, :] = shard[1].astype(BF16)
        copy_of(kind, key, rests_out.at[rows, :], rests_in.at[rows, :], to).start()

    def add_shard(shard, place, mains_in, rests_in):
        return (
            shard[0] + mains_in[pl.ds(place * H, H), :].astype(F32),
            shard[1] + rests_in[blocks(place), :].astype(F32),
        )

    def send_b(d1, d2):
        to = {1: "bp", 2: "b2", 3: "bm"}[d2]
        shard = shard_of(d1, d2)
        send_shard("bo", ("bo", d1), 4 * d2 + d1, shard, b_main, b_rest, b_main_in, b_rest_in, to)

    def raw_inner(slot, carry):
        rows = pl.ds(pl.multiple_of(slot * H, 32), H)
        total = jnp.concatenate(rests(slot), axis=0) * ip[rows, pl.ds(1024, 128)]
        for q in range(4):
            product = rmain[q, rows, :].astype(F32) * ip[rows, pl.ds(256 * q, 256)]
            total = total + product[:, :128] + product[:, 128:]
        high = total.astype(BF16)
        low = (total - high.astype(F32)).astype(BF16)
        rows = pl.ds(pl.multiple_of(slot * 128, 128), H)
        inner_sums[rows, pl.ds(0, 128)] = high
        inner_sums[rows, pl.ds(128, 128)] = low
        return carry

    for d1 in range(4):
        for d2 in (1, 3):
            if d1 not in FORWARD or d2 != (1 if d1 in VIA_P else 3):
                got_i(("i", d1, d2))
    first, second, third = pl.ds(0, 4 * H), pl.ds(4 * H, 2 * H), pl.ds(6 * H, 2 * H)
    normalised(0, 4)
    got("s early", tbuf.at[blocks(0, 5), :])
    coef_of(0, 4, early)
    ip[first, :] = image_sums(0, 4, early)
    late_t(3)
    late_t(5)
    for d1 in (0, 1):
        got_i(("i", d1, 2))
    normalised(4, 2)
    coef_of(4, 2, early)
    late_t(4)
    ip[second, :] = image_sums(4, 2, early)

    got("s late", tbuf.at[blocks(0, 3), :])
    coef_of(0, 4, late)
    ip[first, :] += image_sums(0, 4, late)
    for d1 in (2, 1, 3, 0):
        for d2 in (1, 3):
            send_b(d1, d2)
    coef_of(4, 2, late)
    for d1 in (2, 3):
        got_i(("i", d1, 2))
    normalised(6, 2)
    coef_of(6, 2, late)
    coef_of(6, 2, early)

    def inner_b():
        lax.fori_loop(0, 8, raw_inner, 0)
        along = lax.dot_general(
            jnp.ones((8, 256), BF16), inner_sums[...], (((1,), (1,)), ((), ())), preferred_element_type=F32
        )
        for slot in range(8):
            inner_slots[slot] = along[:, slot * 128:(slot + 1) * 128]
        for d2 in (1, 2, 3):
            for d1 in range(4):
                b_inner[4 * d2 + d1] = inner_slots[slot_of(d1, d2)]
            four = pl.ds(4 * d2, 4)
            to = {1: "bp", 2: "b2", 3: "bm"}[d2]
            copy_of("bi", "bi", b_inner.at[four], b_inner_in.at[four], to).start()

    def send_so(k):
        rows = blocks(k)
        sib_out[rows, :] = tp[blocks(OTHER[k]), :].astype(BF16)
        copy_of("so", ("so", k), sib_out.at[rows, :], sib_in.at[rows, :], "sib").start()

    tp[late[1], :] = text_sums(0, 8, late)
    for k in (4, 5, 3):
        send_so(k)
    tp[early[1], :] = text_sums(0, 8, early)
    for k in (6, 2, 7, 1, 0):
        send_so(k)
    def z_pass(*hops):
        for k, to, new in hops:
            got(("so", k), sib_in.at[blocks(k), :])
        for p in pieces:
            for k, to, new in hops:
                rows = rows_of(k, p)
                total = tp[rows_of(OWN[k], p), :] + sib_in[rows, :].astype(F32)
                if k not in (4, 5):
                    got(("zo", k, p), z_in.at[rows, :])
                    total = total + z_in[rows, :].astype(F32)
                z_out[rows, :] = total.astype(BF16)
                key = ("zo", new) if new in (0, 8) else ("zo", new, p)
                slot = 4 if new == 8 else new
                copy_of("zo", key, z_out.at[rows, :], z_in.at[rows_of(slot, p), :], to).start()

    z_pass((4, "zp", 3), (5, "zm", 6))
    ip[second, :] += image_sums(4, 2, late)
    ip[third, :] = image_sums(6, 2, early) + image_sums(6, 2, late)
    inner_b()
    for d1 in (2, 1, 3, 0):
        send_b(d1, 2)

    def b_sum(d1):
        got(("bo", d1), tbuf.at[blocks(0, 3), :])
        shard = shard_of(d1, 0)
        for d2 in (1, 2, 3):
            shard = add_shard(shard, 4 * d2 + d1, b_main_in, b_rest_in)
        return shard

    def send_a(d1, to):
        send_shard("ao", "ao", d1, b_sum(d1), a_main, a_rest, a_main_in, a_rest_in, to)

    def inner_sum(d1):
        return inner_slots[slot_of(d1, 0)] + b_inner_in[4 + d1] + b_inner_in[8 + d1] + b_inner_in[12 + d1]

    def inner_a():
        got("bi", b_inner.at[pl.ds(4, 12)])
        for d1, to in ((1, "ap"), (2, "a2"), (3, "am")):
            a_inner[d1] = inner_sum(d1)
            copy_of("ai", "ai", a_inner.at[d1], a_inner_in.at[d1], to).start()

    z_pass((3, "zp", 2), (6, "zm", 7))
    send_a(2, "a2")
    z_pass((2, "zp", 1), (7, "zm", 8))
    send_a(1, "ap")
    send_a(3, "am")
    inner_a()
    z_pass((1, "zp", 0))

    def back_norm(unit_rows, scale, inner, direction):
        return scale * (direction - unit_rows * inner)

    own_rows = pl.ds(4 * H, H)
    squares = jnp.concatenate(rests(4), axis=0) ** 2
    for q in range(4):
        part = rmain[q, own_rows, :].astype(F32)
        squares = squares + part[:, :128] ** 2 + part[:, 128:] ** 2
    scale_i = lax.rsqrt(jnp.sum(squares, axis=-1, keepdims=True) + 1e-06)
    unit_main = jnp.concatenate([rmain[2 * xh + i, own_rows, :].astype(F32) for i in (0, 1)], axis=1) * scale_i
    scale_rest = jnp.where(left_side, scale_i[:R], scale_i[R:])
    unit_rest = rrem[xh, blocks(4), :].astype(F32) * scale_rest
    got("ai", a_inner.at[pl.ds(1, 3)])
    along = inner_sum(0) + a_inner_in[1] + a_inner_in[2] + a_inner_in[3]
    inner_i = scale_i * jnp.transpose(jnp.broadcast_to(along[:1], (128, 128)))[:H, :1]
    inner_rest = jnp.where(left_side, inner_i[:R], inner_i[R:])

    shard = b_sum(0)
    got("ao", tbuf.at[blocks(0, 3), :])
    for d1 in (1, 2, 3):
        shard = add_shard(shard, d1, a_main_in, a_rest_in)
    grad = back_norm(unit_main, scale_i, inner_i, shard[0]).astype(BF16)
    g_main[0] = grad[:, :256]
    g_main[1] = grad[:, 256:]
    g_rest[...] = back_norm(unit_rest, scale_rest, inner_rest, shard[1]).astype(BF16)
    copy_of("g", "g", g_main.at[1 - c], g_main_in, "sib").start()
    copy_of("h", "g", g_rest, g_rest_in, "sib").start()

    def put_image(rows, main, rest):
        rest = rest.astype(F32)
        low = jnp.where(c == 0, rest[:, :32], rest[:, 32:64])
        high = jnp.where(c == 0, rest[:, 64:96], rest[:, 96:])
        oimg[rows, pl.ds(0, 256)] = main
        oimg[rows, pl.ds(256, 32)] = jnp.concatenate([low, high], axis=0).astype(BF16)

    put_image(here, g_main[c], g_rest[...])

    got(("so", 0), sib_in.at[blocks(0), :])
    got(("zo", 0), z_in.at[blocks(0), :])
    got(("zo", 8), z_in.at[blocks(4), :])
    direction = tp[blocks(0), :] + sib_in[blocks(0), :].astype(F32)
    direction = direction + z_in[blocks(0), :].astype(F32) + z_in[blocks(4), :].astype(F32)
    text_unit, text_scale = tunit[...], tscales[:, :1]
    text_inner = jnp.sum(text_unit * direction, axis=-1, keepdims=True)
    text_grad = back_norm(text_unit, text_scale, text_inner, direction)
    otxt[...] = jnp.concatenate([quarter(text_grad, j) for j in range(4)], axis=1).astype(BF16)

    left("x", rmain.at[0, pl.ds(0, H), :])
    left("y", xrem)
    left("t", tbuf.at[blocks(0, 7), :])
    left("s", tbuf.at[blocks(0, 8), :])
    left("i", ibuf.at[blocks(0, 15), :])
    left("so", sib_out)
    left("bo", tbuf.at[blocks(0, 12), :])
    left("zo", z_out.at[blocks(0, 7), :])
    left("ao", tbuf.at[blocks(0, 3), :])
    left("bi", b_inner.at[pl.ds(4, 12)])
    left("ai", a_inner.at[pl.ds(1, 3)])
    got("g", rrem.at[0, pl.ds(0, 5 * R), :])
    put_image(there, g_main_in[...], g_rest_in[...])
    left("g", g_main.at[0])
    left("h", g_rest)
    assert (len(send_ids), len(recv_ids)) == (SENDS, RECVS), (len(send_ids), len(recv_ids))


def hand_out(image_grad, text_grad, oimg, otxt, sems):
    copies = [
        pltpu.make_async_copy(image_grad, oimg, sems.at[0]),
        pltpu.make_async_copy(text_grad, otxt, sems.at[1]),
    ]
    for copy in copies:
        copy.start()
    for copy in copies:
        copy.wait()


def on_device(image_features, text_features):
    vmem = pltpu.VMEM
    image_grad, text_grad = pl.pallas_call(
        kernel,
        out_shape=(
            jax.ShapeDtypeStruct((4 * R, Q), BF16),
            jax.ShapeDtypeStruct((R, D), BF16),
        ),
        in_specs=[pl.BlockSpec(memory_space=pl.ANY)] * 2,
        out_specs=(pl.BlockSpec(memory_space=vmem), pl.BlockSpec(memory_space=vmem)),
        scratch_shapes=[
            vmem((4 * R, Q), BF16),
            vmem((R, 128), BF16),
            vmem((R, 128), BF16),
            vmem((4, N, 256), BF16),
            vmem((2, N // 2, 128), BF16),
            vmem((R, D), BF16),
            vmem((R, D), F32),
            vmem((R, 128), F32),
            vmem((N, D), BF16),
            vmem((N, D), BF16),
            vmem((N, EARLY), BF16),
            vmem((N, LATE), BF16),
            vmem((N, D), F32),
            vmem((N, D), F32),
            vmem((8 * R, D), BF16),
            vmem((8 * R, D), BF16),
            vmem((8 * R, D), BF16),
            vmem((8 * R, D), BF16),
            vmem((16 * H, 512), BF16),
            vmem((16 * R, 128), BF16),
            vmem((16 * H, 512), BF16),
            vmem((16 * R, 128), BF16),
            vmem((4 * H, 512), BF16),
            vmem((4 * R, 128), BF16),
            vmem((4 * H, 512), BF16),
            vmem((4 * R, 128), BF16),
            vmem((8 * 128, 256), BF16),
            vmem((8, 8, 128), F32),
            vmem((16, 8, 128), F32),
            vmem((16, 8, 128), F32),
            vmem((4, 8, 128), F32),
            vmem((4, 8, 128), F32),
            vmem((2, H, 256), BF16),
            vmem((R, 128), BF16),
            vmem((H, 256), BF16),
            vmem((R, 128), BF16),
            pltpu.SemaphoreType.DMA((SENDS,)),
            pltpu.SemaphoreType.DMA((RECVS,)),
            pltpu.SemaphoreType.DMA((3,)),
        ],
        compiler_params=pltpu.CompilerParams(
            collective_id=0, has_side_effects=True, vmem_limit_bytes=60 * 1024 * 1024
        ),
        cost_estimate=pl.CostEstimate(
            flops=6 * N * N * D, bytes_accessed=8 * R * D, transcendentals=N * N
        ),
    )(image_features, text_features)
    return pl.pallas_call(
        hand_out,
        out_shape=(
            jax.ShapeDtypeStruct((4 * R, Q), BF16),
            jax.ShapeDtypeStruct((R, D), BF16),
        ),
        in_specs=[pl.BlockSpec(memory_space=pltpu.VMEM)] * 2,
        out_specs=[pl.BlockSpec(memory_space=pltpu.HBM)] * 2,
        scratch_shapes=[pltpu.SemaphoreType.DMA((2,))],
    )(image_grad, text_grad)


def solution(mesh):
    placed = (P("loop", "grp"), P(("loop", "grp"), None))
    return jax.shard_map(
        on_device, mesh=mesh, in_specs=placed, out_specs=placed, check_vma=False
    )
```

```python
import jax
import jax.numpy as jnp
from jax import lax
from jax.experimental import pallas as pl
from jax.experimental.pallas import tpu as pltpu
from jax.sharding import PartitionSpec as P

LOGIT_SCALE = 16.0
LOGIT_BIAS = -4.0
BF16 = jnp.bfloat16
F32 = jnp.float32
H = 96
R = 48
D = 1152
Q = 288
N = 768
PIECES = 3
PR = R // PIECES
SENDS = 13
RECVS = 66
GREETED = ("zp", "zm", "zp2", "zm2", "ap", "am", "bp", "bm", "x2", "y2", "sib")
MESH = pl.DeviceIdType.MESH
FORWARD = (0, 1, 3, 2)
OWN = {0: 0, 1: 1, 7: 2, 2: 3, 6: 4, 3: 10, 5: 11, 4: 12}
OTHER = {k: place + (5 if place < 5 else 3) for k, place in OWN.items()}
EARLY = 10 * R
LATE = N - EARLY
VIA_P = (0, 2)


def neighbours():
    loop = lax.axis_index("loop")
    grp = lax.axis_index("grp")
    z = loop // 8
    x = (grp // 2) * 2 + (loop // 4) % 2
    y = loop % 4
    c = grp % 2

    def dev(dz, dx, dy, flip=0):
        zz = (z + dz + 8) % 8
        xx = (x + dx + 4) % 4
        yy = (y + dy + 4) % 4
        return (zz * 8 + (xx % 2) * 4 + yy, (xx // 2) * 2 + (c + flip) % 2)

    f = 1 - 2 * c
    return {
        "zp": dev(f, 0, 0),
        "zm": dev(-f, 0, 0),
        "zp2": dev(2 * f, 0, 0),
        "zm2": dev(-2 * f, 0, 0),
        "ap": dev(0, 1 - c, c),
        "am": dev(0, c - 1, -c),
        "bp": dev(0, c, 1 - c),
        "bm": dev(0, -c, c - 1),
        "a2": dev(0, 2 - 2 * c, 2 * c),
        "b2": dev(0, 2 * c, 2 - 2 * c),
        "x2": dev(0, 2, 0),
        "y2": dev(0, 0, 2),
        "sib": dev(0, 0, 0, 1),
    }, grp, x, c


def unit_of(values):
    scale = lax.rsqrt(jnp.sum(values * values, axis=-1, keepdims=True) + 1e-06)
    return values * scale, scale


def permuted(values):
    mains = [values[:, q * Q:q * Q + 256] for q in range(4)]
    return jnp.concatenate(mains + [values[:, q * Q + 256:(q + 1) * Q] for q in range(4)], axis=1)


def quarter(values, q):
    return jnp.concatenate(
        [values[:, q * 256:(q + 1) * 256], values[:, 1024 + q * 32:1024 + (q + 1) * 32]], axis=1
    )


def kernel(
    img, txt, oimg, otxt,
    ximg, xrem, srem, rmain, rrem, tin, tunit, tscales, ibuf, tbuf, coef_early, coef_late, ip, tp,
    sib_out, sib_in, z_out, z_in, b_main, b_rest, b_main_in, b_rest_in, a_main, a_rest, a_main_in, a_rest_in,
    inner_sums, inner_slots, b_inner, b_inner_in, a_inner, a_inner_in, g_main, g_rest, g_main_in, g_rest_in,
    send_sems, recv_sems, local_sems,
):
    dev, grp, x, c = neighbours()
    xh = x // 2
    send_ids = {}
    recv_ids = {}

    def copy_of(kind, key, src, dst, to):
        out = send_ids.setdefault(kind, len(send_ids))
        arrive = recv_ids.setdefault(key, len(recv_ids))
        return pltpu.make_async_remote_copy(
            src_ref=src, dst_ref=dst, send_sem=send_sems.at[out],
            recv_sem=recv_sems.at[arrive], device_id=dev[to], device_id_type=MESH,
        )

    def got(key, ref):
        pltpu.make_async_copy(ref, ref, recv_sems.at[recv_ids[key]]).wait()

    def left(kind, ref):
        pltpu.make_async_copy(ref, ref, send_sems.at[send_ids[kind]]).wait()

    def blocks(slot, count=1):
        return pl.ds(slot * R, count * R)

    def rows_of(slot, piece):
        return pl.ds(slot * R + piece * PR, PR)

    pieces = range(PIECES)
    load_t = pltpu.make_async_copy(txt, tin, local_sems.at[0])
    load_t.start()
    load_i = pltpu.make_async_copy(img, ximg, local_sems.at[1])
    load_i.start()

    barrier = pltpu.get_barrier_semaphore()
    for name in GREETED:
        pl.semaphore_signal(barrier, inc=1, device_id=dev[name], device_id_type=MESH)
    load_t.wait()
    unit, tscale = unit_of(permuted(tin[...].astype(F32)))
    tbuf[blocks(0), :] = unit.astype(BF16)
    tunit[...] = unit
    tscales[...] = jnp.broadcast_to(tscale, (R, 128))
    inner_sums[...] = jnp.zeros_like(inner_sums)
    load_i.wait()

    def rest_of(half):
        rest = ximg[pl.ds(pl.multiple_of(half * H, 32), H), 256:].astype(F32)
        low, high = rest[:R], rest[R:]
        gap = jnp.zeros_like(low)
        return jnp.where(
            c == 0,
            jnp.concatenate([low, gap, high, gap], axis=1),
            jnp.concatenate([gap, low, gap, high], axis=1),
        )

    xrem[...] = rest_of(1 - c).astype(BF16)
    rest_here = rest_of(c)
    there = pl.ds(pl.multiple_of((1 - c) * H, 32), H)
    here = pl.ds(pl.multiple_of(c * H, 32), H)
    rmain[grp, pl.ds(4 * H, H), :] = ximg[here, :256]
    pl.semaphore_wait(barrier, len(GREETED))

    def send_t(to, slot, new, piece):
        key = ("t", new) if new in (3, 4, 5) else ("t", new, piece)
        src, dst = rows_of(OWN[slot], piece), rows_of(OWN[new], piece)
        copy_of("t", key, tbuf.at[src, :], tbuf.at[dst, :], to).start()

    def send_s(slot):
        key = "s late" if slot in (3, 5, 4) else "s early"
        src, dst = blocks(OWN[slot]), blocks(OTHER[slot])
        copy_of("s", key, tbuf.at[src, :], tbuf.at[dst, :], "sib").start()

    for p in pieces:
        send_t("zm", 0, 1, p)
        send_t("zp", 0, 7, p)

    copy_of("x", "x", ximg.at[there, pl.ds(0, 256)], rmain.at[grp, pl.ds(4 * H, H), :], "sib").start()
    copy_of("y", "x", xrem, srem, "sib").start()
    send_s(0)

    def slot_of(d1, d2):
        return 4 * (1 - d2 % 2) + (1 - c) * ((d2 // 2) * 2 + d1 % 2) + c * d1

    def half_of(d1, d2):
        return ((x + (1 - c) * d1 + c * d2) % 4) // 2

    def send_i(to, source, target, key):
        half = half_of(*source)
        quarters = pl.ds(2 * half, 2)
        came, goes = slot_of(*source), slot_of(*target)
        src = pl.ds(pl.multiple_of(came * H, 32), H)
        dst = pl.ds(pl.multiple_of(goes * H, 32), H)
        copy_of("i", key, rmain.at[quarters, src, :], rmain.at[quarters, dst, :], to).start()
        src = pl.ds(pl.multiple_of(came * R, 16), R)
        dst = pl.ds(pl.multiple_of(goes * R, 16), R)
        copy_of("i", key, rrem.at[half, src, :], rrem.at[half, dst, :], to).start()

    def got_i(key):
        got(key, tbuf.at[blocks(0), :])

    def near_b(d1):
        send_i("bm", (d1, 0), (d1, 1), ("i", d1, 1))
        send_i("bp", (d1, 0), (d1, 3), ("i", d1, 3))
        if d1 not in FORWARD:
            send_i("b2", (d1, 0), (d1, 2), ("i", d1, 2))

    def far_b(d1):
        if d1 in VIA_P:
            got_i(("i", d1, 1))
            send_i("bm", (d1, 1), (d1, 2), ("i", d1, 2))
        else:
            got_i(("i", d1, 3))
            send_i("bp", (d1, 3), (d1, 2), ("i", d1, 2))

    got("x", rrem.at[0, pl.ds(0, 5 * R), :])
    rrem[xh, pl.ds(4 * R, R), :] = (rest_here + srem[...].astype(F32)).astype(BF16)
    send_i("am", (0, 0), (1, 0), ("i", 1, 0))
    send_i("ap", (0, 0), (3, 0), ("i", 3, 0))
    near_b(0)
    send_i("a2", (0, 0), (2, 0), ("i", 2, 0))

    def ring_t(new_m, new_p):
        for p in pieces:
            got(("t", new_m, p), tbuf.at[rows_of(OWN[new_m], p), :])
            send_t("zm", new_m, new_m + 1, p)
            if new_p == 6:
                send_t("zm2", 2, 4, p)
            got(("t", new_p, p), tbuf.at[rows_of(OWN[new_p], p), :])
            send_t("zp", new_p, new_p - 1, p)
        send_s(new_m)
        send_s(new_p)

    ring_t(1, 7)
    for d1 in (1, 3):
        got_i(("i", d1, 0))
        near_b(d1)
    got_i(("i", 2, 0))
    near_b(2)
    ring_t(2, 6)
    for d1 in FORWARD:
        far_b(d1)

    def late_t(slot):
        got(("t", slot), tbuf.at[blocks(OWN[slot]), :])
        send_s(slot)

    def rests(slot):
        rows = pl.ds(pl.multiple_of(slot * R, 16), R)
        first, second = rrem[0, rows, :].astype(F32), rrem[1, rows, :].astype(F32)
        left_side = lax.broadcasted_iota(jnp.int32, first.shape, 1) < 64
        low = jnp.where(left_side, first, pltpu.roll(second, 64, 1))
        high = jnp.where(left_side, pltpu.roll(first, 64, 1), second)
        return low, high

    def normalise(slot, carry):
        rows = pl.ds(pl.multiple_of(slot * H, 32), H)
        parts = [rmain[q, rows, :].astype(F32) for q in range(4)]
        parts.append(jnp.concatenate(rests(slot), axis=0))
        squares = [jnp.sum(part * part, axis=-1, keepdims=True) for part in parts]
        scale = lax.rsqrt(sum(squares[1:], squares[0]) + 1e-06)
        for q, part in enumerate(parts):
            ibuf[rows, pl.ds(256 * q, part.shape[1])] = (part * scale).astype(BF16)
        return carry

    def normalised(slot, count):
        lax.fori_loop(slot, slot + count, normalise, 0)

    def coef_of(slot, count, part):
        store, texts = part
        rows = pl.ds(slot * H, count * H)
        logits = LOGIT_SCALE * lax.dot_general(
            ibuf[rows, :], tbuf[texts, :], (((1,), (1,)), ((), ())), preferred_element_type=F32
        ) + LOGIT_BIAS
        chance = jax.nn.sigmoid(logits)
        if slot == 4 and part is early:
            row_ids = lax.broadcasted_iota(jnp.int32, chance.shape, 0)
            col_ids = lax.broadcasted_iota(jnp.int32, chance.shape, 1)
            start = OTHER[0] * R
            own = (col_ids < R) & (row_ids == col_ids + c * R)
            other = (col_ids >= start) & (col_ids < start + R) & (row_ids == col_ids - start + (1 - c) * R)
            chance = chance - jnp.where((own | other) & (c == xh), 1.0, 0.0)
        store[rows, :] = (LOGIT_SCALE * chance).astype(BF16)

    def image_sums(slot, count, part):
        store, texts = part
        rows = pl.ds(slot * H, count * H)
        return jnp.dot(store[rows, :], tbuf[texts, :], preferred_element_type=F32)

    def text_sums(slot, count, part):
        rows = pl.ds(slot * H, count * H)
        return lax.dot_general(
            part[0][rows, :], ibuf[rows, :], (((0,), (0,)), ((), ())), preferred_element_type=F32
        )

    early = (coef_early, pl.ds(0, EARLY))
    late = (coef_late, pl.ds(EARLY, LATE))

    left_side = lax.broadcasted_iota(jnp.int32, (R, 128), 1) < 64

    def shard_of(d1, d2):
        rows = pl.ds(pl.multiple_of(slot_of(d1, d2) * H, 32), H)
        half = half_of(d1, d2)
        main = ip[rows, pl.ds(pl.multiple_of(half * 512, 512), 512)]
        low, high = ip[rows, pl.ds(1024, 128)][:R], ip[rows, pl.ds(1024, 128)][R:]
        rest = jnp.where(
            half == 0,
            jnp.where(left_side, low, pltpu.roll(high, 64, 1)),
            jnp.where(left_side, pltpu.roll(low, 64, 1), high),
        )
        return main, rest

    def send_shard(kind, key, place, shard, mains, rests_out, mains_in, rests_in, to):
        rows = pl.ds(place * H, H)
        mains[rows, :] = shard[0].astype(BF16)
        copy_of(kind, key, mains.at[rows, :], mains_in.at[rows, :], to).start()
        rows = blocks(place)
        rests_out[rows, :] = shard[1].astype(BF16)
        copy_of(kind, key, rests_out.at[rows, :], rests_in.at[rows, :], to).start()

    def add_shard(shard, place, mains_in, rests_in):
        return (
            shard[0] + mains_in[pl.ds(place * H, H), :].astype(F32),
            shard[1] + rests_in[blocks(place), :].astype(F32),
        )

    def send_b(d1, d2):
        to = {1: "bp", 2: "b2", 3: "bm"}[d2]
        shard = shard_of(d1, d2)
        send_shard("bo", ("bo", d1), 4 * d2 + d1, shard, b_main, b_rest, b_main_in, b_rest_in, to)

    def raw_inner(slot, carry):
        rows = pl.ds(pl.multiple_of(slot * H, 32), H)
        total = jnp.concatenate(rests(slot), axis=0) * ip[rows, pl.ds(1024, 128)]
        for q in range(4):
            product = rmain[q, rows, :].astype(F32) * ip[rows, pl.ds(256 * q, 256)]
            total = total + product[:, :128] + product[:, 128:]
        high = total.astype(BF16)
        low = (total - high.astype(F32)).astype(BF16)
        rows = pl.ds(pl.multiple_of(slot * 128, 128), H)
        inner_sums[rows, pl.ds(0, 128)] = high
        inner_sums[rows, pl.ds(128, 128)] = low
        return carry

    for d1 in range(4):
        for d2 in (1, 3):
            if d1 not in FORWARD or d2 != (1 if d1 in VIA_P else 3):
                got_i(("i", d1, d2))
    first, second = pl.ds(0, 4 * H), pl.ds(4 * H, 4 * H)
    normalised(0, 4)
    got("s early", tbuf.at[blocks(0, 5), :])
    coef_of(0, 4, early)
    ip[first, :] = image_sums(0, 4, early)
    late_t(3)
    late_t(5)
    for d1 in (0, 1):
        got_i(("i", d1, 2))
    normalised(4, 2)
    coef_of(4, 2, early)
    late_t(4)

    got("s late", tbuf.at[blocks(0, 3), :])
    coef_of(0, 4, late)
    ip[first, :] += image_sums(0, 4, late)
    for d1 in (2, 1, 3, 0):
        for d2 in (1, 3):
            send_b(d1, d2)
    coef_of(4, 2, late)
    for d1 in (2, 3):
        got_i(("i", d1, 2))
    normalised(6, 2)
    coef_of(6, 2, late)
    coef_of(6, 2, early)

    def inner_b():
        lax.fori_loop(0, 8, raw_inner, 0)
        along = lax.dot_general(
            jnp.ones((8, 256), BF16), inner_sums[...], (((1,), (1,)), ((), ())), preferred_element_type=F32
        )
        for slot in range(8):
            inner_slots[slot] = along[:, slot * 128:(slot + 1) * 128]
        for d2 in (1, 2, 3):
            for d1 in range(4):
                b_inner[4 * d2 + d1] = inner_slots[slot_of(d1, d2)]
            four = pl.ds(4 * d2, 4)
            to = {1: "bp", 2: "b2", 3: "bm"}[d2]
            copy_of("bi", "bi", b_inner.at[four], b_inner_in.at[four], to).start()

    def send_so(k):
        rows = blocks(k)
        sib_out[rows, :] = tp[blocks(OTHER[k]), :].astype(BF16)
        copy_of("so", ("so", k), sib_out.at[rows, :], sib_in.at[rows, :], "sib").start()

    tp[late[1], :] = text_sums(0, 8, late)
    for k in (4, 5, 3):
        send_so(k)
    tp[early[1], :] = text_sums(0, 8, early)
    for k in (6, 2, 7, 1, 0):
        send_so(k)
    def z_pass(*hops):
        for k, to, new in hops:
            got(("so", k), sib_in.at[blocks(k), :])
        for p in pieces:
            for k, to, new in hops:
                rows = rows_of(k, p)
                total = tp[rows_of(OWN[k], p), :] + sib_in[rows, :].astype(F32)
                if k not in (4, 5):
                    got(("zo", k, p), z_in.at[rows, :])
                    total = total + z_in[rows, :].astype(F32)
                z_out[rows, :] = total.astype(BF16)
                key = ("zo", new) if new in (0, 8) else ("zo", new, p)
                slot = 4 if new == 8 else new
                copy_of("zo", key, z_out.at[rows, :], z_in.at[rows_of(slot, p), :], to).start()

    z_pass((4, "zp", 3), (5, "zm", 6))
    ip[second, :] = image_sums(4, 4, early) + image_sums(4, 4, late)
    inner_b()
    for d1 in (2, 1, 3, 0):
        send_b(d1, 2)

    def b_sum(d1):
        got(("bo", d1), tbuf.at[blocks(0, 3), :])
        shard = shard_of(d1, 0)
        for d2 in (1, 2, 3):
            shard = add_shard(shard, 4 * d2 + d1, b_main_in, b_rest_in)
        return shard

    def send_a(d1, to):
        send_shard("ao", "ao", d1, b_sum(d1), a_main, a_rest, a_main_in, a_rest_in, to)

    def inner_sum(d1):
        return inner_slots[slot_of(d1, 0)] + b_inner_in[4 + d1] + b_inner_in[8 + d1] + b_inner_in[12 + d1]

    def inner_a():
        got("bi", b_inner.at[pl.ds(4, 12)])
        for d1, to in ((1, "ap"), (2, "a2"), (3, "am")):
            a_inner[d1] = inner_sum(d1)
            copy_of("ai", "ai", a_inner.at[d1], a_inner_in.at[d1], to).start()

    z_pass((3, "zp", 2), (6, "zm", 7))
    send_a(2, "a2")
    z_pass((2, "zp", 1), (7, "zm", 8))
    send_a(1, "ap")
    send_a(3, "am")
    inner_a()
    z_pass((1, "zp", 0))

    def back_norm(unit_rows, scale, inner, direction):
        return scale * (direction - unit_rows * inner)

    own_rows = pl.ds(4 * H, H)
    squares = jnp.concatenate(rests(4), axis=0) ** 2
    for q in range(4):
        part = rmain[q, own_rows, :].astype(F32)
        squares = squares + part[:, :128] ** 2 + part[:, 128:] ** 2
    scale_i = lax.rsqrt(jnp.sum(squares, axis=-1, keepdims=True) + 1e-06)
    unit_main = jnp.concatenate([rmain[2 * xh + i, own_rows, :].astype(F32) for i in (0, 1)], axis=1) * scale_i
    scale_rest = jnp.where(left_side, scale_i[:R], scale_i[R:])
    unit_rest = rrem[xh, blocks(4), :].astype(F32) * scale_rest
    got("ai", a_inner.at[pl.ds(1, 3)])
    along = inner_sum(0) + a_inner_in[1] + a_inner_in[2] + a_inner_in[3]
    inner_i = scale_i * jnp.transpose(jnp.broadcast_to(along[:1], (128, 128)))[:H, :1]
    inner_rest = jnp.where(left_side, inner_i[:R], inner_i[R:])

    shard = b_sum(0)
    got("ao", tbuf.at[blocks(0, 3), :])
    for d1 in (1, 2, 3):
        shard = add_shard(shard, d1, a_main_in, a_rest_in)
    grad = back_norm(unit_main, scale_i, inner_i, shard[0]).astype(BF16)
    g_main[0] = grad[:, :256]
    g_main[1] = grad[:, 256:]
    g_rest[...] = back_norm(unit_rest, scale_rest, inner_rest, shard[1]).astype(BF16)
    copy_of("g", "g", g_main.at[1 - c], g_main_in, "sib").start()
    copy_of("h", "g", g_rest, g_rest_in, "sib").start()

    def put_image(rows, main, rest):
        rest = rest.astype(F32)
        low = jnp.where(c == 0, rest[:, :32], rest[:, 32:64])
        high = jnp.where(c == 0, rest[:, 64:96], rest[:, 96:])
        oimg[rows, pl.ds(0, 256)] = main
        oimg[rows, pl.ds(256, 32)] = jnp.concatenate([low, high], axis=0).astype(BF16)

    put_image(here, g_main[c], g_rest[...])

    got(("so", 0), sib_in.at[blocks(0), :])
    got(("zo", 0), z_in.at[blocks(0), :])
    got(("zo", 8), z_in.at[blocks(4), :])
    direction = tp[blocks(0), :] + sib_in[blocks(0), :].astype(F32)
    direction = direction + z_in[blocks(0), :].astype(F32) + z_in[blocks(4), :].astype(F32)
    text_unit, text_scale = tunit[...], tscales[:, :1]
    text_inner = jnp.sum(text_unit * direction, axis=-1, keepdims=True)
    text_grad = back_norm(text_unit, text_scale, text_inner, direction)
    otxt[...] = jnp.concatenate([quarter(text_grad, j) for j in range(4)], axis=1).astype(BF16)

    left("x", rmain.at[0, pl.ds(0, H), :])
    left("y", xrem)
    left("t", tbuf.at[blocks(0, 7), :])
    left("s", tbuf.at[blocks(0, 8), :])
    left("i", ibuf.at[blocks(0, 15), :])
    left("so", sib_out)
    left("bo", tbuf.at[blocks(0, 12), :])
    left("zo", z_out.at[blocks(0, 7), :])
    left("ao", tbuf.at[blocks(0, 3), :])
    left("bi", b_inner.at[pl.ds(4, 12)])
    left("ai", a_inner.at[pl.ds(1, 3)])
    got("g", rrem.at[0, pl.ds(0, 5 * R), :])
    put_image(there, g_main_in[...], g_rest_in[...])
    left("g", g_main.at[0])
    left("h", g_rest)
    assert (len(send_ids), len(recv_ids)) == (SENDS, RECVS), (len(send_ids), len(recv_ids))


def hand_out(image_grad, text_grad, oimg, otxt, sems):
    copies = [
        pltpu.make_async_copy(image_grad, oimg, sems.at[0]),
        pltpu.make_async_copy(text_grad, otxt, sems.at[1]),
    ]
    for copy in copies:
        copy.start()
    for copy in copies:
        copy.wait()


def on_device(image_features, text_features):
    vmem = pltpu.VMEM
    image_grad, text_grad = pl.pallas_call(
        kernel,
        out_shape=(
            jax.ShapeDtypeStruct((4 * R, Q), BF16),
            jax.ShapeDtypeStruct((R, D), BF16),
        ),
        in_specs=[pl.BlockSpec(memory_space=pl.ANY)] * 2,
        out_specs=(pl.BlockSpec(memory_space=vmem), pl.BlockSpec(memory_space=vmem)),
        scratch_shapes=[
            vmem((4 * R, Q), BF16),
            vmem((R, 128), BF16),
            vmem((R, 128), BF16),
            vmem((4, N, 256), BF16),
            vmem((2, N // 2, 128), BF16),
            vmem((R, D), BF16),
            vmem((R, D), F32),
            vmem((R, 128), F32),
            vmem((N, D), BF16),
            vmem((N, D), BF16),
            vmem((N, EARLY), BF16),
            vmem((N, LATE), BF16),
            vmem((N, D), F32),
            vmem((N, D), F32),
            vmem((8 * R, D), BF16),
            vmem((8 * R, D), BF16),
            vmem((8 * R, D), BF16),
            vmem((8 * R, D), BF16),
            vmem((16 * H, 512), BF16),
            vmem((16 * R, 128), BF16),
            vmem((16 * H, 512), BF16),
            vmem((16 * R, 128), BF16),
            vmem((4 * H, 512), BF16),
            vmem((4 * R, 128), BF16),
            vmem((4 * H, 512), BF16),
            vmem((4 * R, 128), BF16),
            vmem((8 * 128, 256), BF16),
            vmem((8, 8, 128), F32),
            vmem((16, 8, 128), F32),
            vmem((16, 8, 128), F32),
            vmem((4, 8, 128), F32),
            vmem((4, 8, 128), F32),
            vmem((2, H, 256), BF16),
            vmem((R, 128), BF16),
            vmem((H, 256), BF16),
            vmem((R, 128), BF16),
            pltpu.SemaphoreType.DMA((SENDS,)),
            pltpu.SemaphoreType.DMA((RECVS,)),
            pltpu.SemaphoreType.DMA((3,)),
        ],
        compiler_params=pltpu.CompilerParams(
            collective_id=0, has_side_effects=True, vmem_limit_bytes=60 * 1024 * 1024
        ),
        cost_estimate=pl.CostEstimate(
            flops=6 * N * N * D, bytes_accessed=8 * R * D, transcendentals=N * N
        ),
    )(image_features, text_features)
    return pl.pallas_call(
        hand_out,
        out_shape=(
            jax.ShapeDtypeStruct((4 * R, Q), BF16),
            jax.ShapeDtypeStruct((R, D), BF16),
        ),
        in_specs=[pl.BlockSpec(memory_space=pltpu.VMEM)] * 2,
        out_specs=[pl.BlockSpec(memory_space=pltpu.HBM)] * 2,
        scratch_shapes=[pltpu.SemaphoreType.DMA((2,))],
    )(image_grad, text_grad)


def solution(mesh):
    placed = (P("loop", "grp"), P(("loop", "grp"), None))
    return jax.shard_map(
        on_device, mesh=mesh, in_specs=placed, out_specs=placed, check_vma=False
    )
```

```python
import jax
import jax.numpy as jnp
from jax import lax
from jax.experimental import pallas as pl
from jax.experimental.pallas import tpu as pltpu
from jax.sharding import PartitionSpec as P

LOGIT_SCALE = 16.0
LOGIT_BIAS = -4.0
BF16 = jnp.bfloat16
F32 = jnp.float32
H = 96
R = 48
D = 1152
Q = 288
N = 768
PIECES = 3
PR = R // PIECES
SENDS = 13
RECVS = 66
GREETED = ("zp", "zm", "zp2", "zm2", "ap", "am", "bp", "bm", "x2", "y2", "sib")
MESH = pl.DeviceIdType.MESH
FORWARD = (0, 1, 3, 2)
OWN = {0: 0, 1: 1, 7: 2, 2: 3, 6: 4, 3: 10, 5: 11, 4: 12}
OTHER = {k: place + (5 if place < 5 else 3) for k, place in OWN.items()}
EARLY = 10 * R
LATE = N - EARLY
VIA_P = (0, 2)


def neighbours():
    loop = lax.axis_index("loop")
    grp = lax.axis_index("grp")
    z = loop // 8
    x = (grp // 2) * 2 + (loop // 4) % 2
    y = loop % 4
    c = grp % 2

    def dev(dz, dx, dy, flip=0):
        zz = (z + dz + 8) % 8
        xx = (x + dx + 4) % 4
        yy = (y + dy + 4) % 4
        return (zz * 8 + (xx % 2) * 4 + yy, (xx // 2) * 2 + (c + flip) % 2)

    f = 1 - 2 * c
    return {
        "zp": dev(f, 0, 0),
        "zm": dev(-f, 0, 0),
        "zp2": dev(2 * f, 0, 0),
        "zm2": dev(-2 * f, 0, 0),
        "ap": dev(0, 1 - c, c),
        "am": dev(0, c - 1, -c),
        "bp": dev(0, c, 1 - c),
        "bm": dev(0, -c, c - 1),
        "a2": dev(0, 2 - 2 * c, 2 * c),
        "b2": dev(0, 2 * c, 2 - 2 * c),
        "x2": dev(0, 2, 0),
        "y2": dev(0, 0, 2),
        "sib": dev(0, 0, 0, 1),
    }, grp, x, c


def unit_of(values):
    scale = lax.rsqrt(jnp.sum(values * values, axis=-1, keepdims=True) + 1e-06)
    return values * scale, scale


def permuted(values):
    mains = [values[:, q * Q:q * Q + 256] for q in range(4)]
    return jnp.concatenate(mains + [values[:, q * Q + 256:(q + 1) * Q] for q in range(4)], axis=1)


def quarter(values, q):
    return jnp.concatenate(
        [values[:, q * 256:(q + 1) * 256], values[:, 1024 + q * 32:1024 + (q + 1) * 32]], axis=1
    )


def kernel(
    img, txt, oimg, otxt,
    ximg, xrem, srem, rmain, rrem, tin, tunit, tscales, ibuf, tbuf, coef_early, coef_late, ip, tp,
    sib_out, sib_in, z_out, z_in, b_main, b_rest, b_main_in, b_rest_in, a_main, a_rest, a_main_in, a_rest_in,
    inner_sums, inner_slots, b_inner, b_inner_in, a_inner, a_inner_in, g_main, g_rest, g_main_in, g_rest_in,
    send_sems, recv_sems, local_sems,
):
    dev, grp, x, c = neighbours()
    xh = x // 2
    send_ids = {}
    recv_ids = {}

    def copy_of(kind, key, src, dst, to):
        out = send_ids.setdefault(kind, len(send_ids))
        arrive = recv_ids.setdefault(key, len(recv_ids))
        return pltpu.make_async_remote_copy(
            src_ref=src, dst_ref=dst, send_sem=send_sems.at[out],
            recv_sem=recv_sems.at[arrive], device_id=dev[to], device_id_type=MESH,
        )

    def got(key, ref):
        pltpu.make_async_copy(ref, ref, recv_sems.at[recv_ids[key]]).wait()

    def left(kind, ref):
        pltpu.make_async_copy(ref, ref, send_sems.at[send_ids[kind]]).wait()

    def blocks(slot, count=1):
        return pl.ds(slot * R, count * R)

    def rows_of(slot, piece):
        return pl.ds(slot * R + piece * PR, PR)

    pieces = range(PIECES)
    load_t = pltpu.make_async_copy(txt, tin, local_sems.at[0])
    load_t.start()
    load_i = pltpu.make_async_copy(img, ximg, local_sems.at[1])
    load_i.start()

    barrier = pltpu.get_barrier_semaphore()
    for name in GREETED:
        pl.semaphore_signal(barrier, inc=1, device_id=dev[name], device_id_type=MESH)
    load_t.wait()
    unit, tscale = unit_of(permuted(tin[...].astype(F32)))
    tbuf[blocks(0), :] = unit.astype(BF16)
    tunit[...] = unit
    tscales[...] = jnp.broadcast_to(tscale, (R, 128))
    inner_sums[...] = jnp.zeros_like(inner_sums)
    load_i.wait()

    def rest_of(half):
        rest = ximg[pl.ds(pl.multiple_of(half * H, 32), H), 256:].astype(F32)
        low, high = rest[:R], rest[R:]
        gap = jnp.zeros_like(low)
        return jnp.where(
            c == 0,
            jnp.concatenate([low, gap, high, gap], axis=1),
            jnp.concatenate([gap, low, gap, high], axis=1),
        )

    xrem[...] = rest_of(1 - c).astype(BF16)
    rest_here = rest_of(c)
    there = pl.ds(pl.multiple_of((1 - c) * H, 32), H)
    here = pl.ds(pl.multiple_of(c * H, 32), H)
    rmain[grp, pl.ds(4 * H, H), :] = ximg[here, :256]
    pl.semaphore_wait(barrier, len(GREETED))

    def send_t(to, slot, new, piece):
        key = ("t", new) if new in (3, 4, 5) else ("t", new, piece)
        src, dst = rows_of(OWN[slot], piece), rows_of(OWN[new], piece)
        copy_of("t", key, tbuf.at[src, :], tbuf.at[dst, :], to).start()

    def send_s(slot):
        key = "s late" if slot in (3, 5, 4) else "s early"
        src, dst = blocks(OWN[slot]), blocks(OTHER[slot])
        copy_of("s", key, tbuf.at[src, :], tbuf.at[dst, :], "sib").start()

    for p in pieces:
        send_t("zm", 0, 1, p)
        send_t("zp", 0, 7, p)

    copy_of("x", "x", ximg.at[there, pl.ds(0, 256)], rmain.at[grp, pl.ds(4 * H, H), :], "sib").start()
    copy_of("y", "x", xrem, srem, "sib").start()
    send_s(0)

    def slot_of(d1, d2):
        return 4 * (1 - d2 % 2) + (1 - c) * ((d2 // 2) * 2 + d1 % 2) + c * d1

    def half_of(d1, d2):
        return ((x + (1 - c) * d1 + c * d2) % 4) // 2

    def send_i(to, source, target, key):
        half = half_of(*source)
        quarters = pl.ds(2 * half, 2)
        came, goes = slot_of(*source), slot_of(*target)
        src = pl.ds(pl.multiple_of(came * H, 32), H)
        dst = pl.ds(pl.multiple_of(goes * H, 32), H)
        copy_of("i", key, rmain.at[quarters, src, :], rmain.at[quarters, dst, :], to).start()
        src = pl.ds(pl.multiple_of(came * R, 16), R)
        dst = pl.ds(pl.multiple_of(goes * R, 16), R)
        copy_of("i", key, rrem.at[half, src, :], rrem.at[half, dst, :], to).start()

    first_hops = (
        ("am", (1, 0), ("i", 1, 0)), ("ap", (3, 0), ("i", 3, 0)),
        ("bm", (0, 1), ("i", 0, 1)), ("bp", (0, 3), ("i", 0, 3)), ("a2", (2, 0), ("i", 2, 0)),
    )

    def send_quarter(to, target, key, q):
        dst = pl.ds(pl.multiple_of(slot_of(*target) * H, 32), H)
        copy_of("i", key, rmain.at[q, pl.ds(4 * H, H), :], rmain.at[q, dst, :], to).start()

    def send_rest(to, target, key):
        dst = pl.ds(pl.multiple_of(slot_of(*target) * R, 16), R)
        copy_of("i", key, rrem.at[xh, blocks(4), :], rrem.at[xh, dst, :], to).start()

    def got_i(key):
        got(key, tbuf.at[blocks(0), :])

    def near_b(d1):
        send_i("bm", (d1, 0), (d1, 1), ("i", d1, 1))
        send_i("bp", (d1, 0), (d1, 3), ("i", d1, 3))
        if d1 not in FORWARD:
            send_i("b2", (d1, 0), (d1, 2), ("i", d1, 2))

    def far_b(d1):
        if d1 in VIA_P:
            got_i(("i", d1, 1))
            send_i("bm", (d1, 1), (d1, 2), ("i", d1, 2))
        else:
            got_i(("i", d1, 3))
            send_i("bp", (d1, 3), (d1, 2), ("i", d1, 2))

    for hop in first_hops:
        send_quarter(*hop, grp)
    got("x", rrem.at[0, pl.ds(0, 5 * R), :])
    rrem[xh, pl.ds(4 * R, R), :] = (rest_here + srem[...].astype(F32)).astype(BF16)
    for hop in first_hops:
        send_quarter(*hop, 2 * xh + 1 - c)
        send_rest(*hop)

    def ring_t(new_m, new_p):
        for p in pieces:
            got(("t", new_m, p), tbuf.at[rows_of(OWN[new_m], p), :])
            send_t("zm", new_m, new_m + 1, p)
            if new_p == 6:
                send_t("zm2", 2, 4, p)
            got(("t", new_p, p), tbuf.at[rows_of(OWN[new_p], p), :])
            send_t("zp", new_p, new_p - 1, p)
        send_s(new_m)
        send_s(new_p)

    ring_t(1, 7)
    for d1 in (1, 3):
        got_i(("i", d1, 0))
        near_b(d1)
    got_i(("i", 2, 0))
    near_b(2)
    ring_t(2, 6)
    for d1 in FORWARD:
        far_b(d1)

    def late_t(slot):
        got(("t", slot), tbuf.at[blocks(OWN[slot]), :])
        send_s(slot)

    def rests(slot):
        rows = pl.ds(pl.multiple_of(slot * R, 16), R)
        first, second = rrem[0, rows, :].astype(F32), rrem[1, rows, :].astype(F32)
        left_side = lax.broadcasted_iota(jnp.int32, first.shape, 1) < 64
        low = jnp.where(left_side, first, pltpu.roll(second, 64, 1))
        high = jnp.where(left_side, pltpu.roll(first, 64, 1), second)
        return low, high

    def normalise(slot, carry):
        rows = pl.ds(pl.multiple_of(slot * H, 32), H)
        parts = [rmain[q, rows, :].astype(F32) for q in range(4)]
        parts.append(jnp.concatenate(rests(slot), axis=0))
        squares = [jnp.sum(part * part, axis=-1, keepdims=True) for part in parts]
        scale = lax.rsqrt(sum(squares[1:], squares[0]) + 1e-06)
        for q, part in enumerate(parts):
            ibuf[rows, pl.ds(256 * q, part.shape[1])] = (part * scale).astype(BF16)
        return carry

    def normalised(slot, count):
        lax.fori_loop(slot, slot + count, normalise, 0)

    def coef_of(slot, count, part):
        store, texts = part
        rows = pl.ds(slot * H, count * H)
        logits = LOGIT_SCALE * lax.dot_general(
            ibuf[rows, :], tbuf[texts, :], (((1,), (1,)), ((), ())), preferred_element_type=F32
        ) + LOGIT_BIAS
        chance = jax.nn.sigmoid(logits)
        if slot == 4 and part is early:
            row_ids = lax.broadcasted_iota(jnp.int32, chance.shape, 0)
            col_ids = lax.broadcasted_iota(jnp.int32, chance.shape, 1)
            start = OTHER[0] * R
            own = (col_ids < R) & (row_ids == col_ids + c * R)
            other = (col_ids >= start) & (col_ids < start + R) & (row_ids == col_ids - start + (1 - c) * R)
            chance = chance - jnp.where((own | other) & (c == xh), 1.0, 0.0)
        store[rows, :] = (LOGIT_SCALE * chance).astype(BF16)

    def image_sums(slot, count, part):
        store, texts = part
        rows = pl.ds(slot * H, count * H)
        return jnp.dot(store[rows, :], tbuf[texts, :], preferred_element_type=F32)

    def text_sums(slot, count, part):
        rows = pl.ds(slot * H, count * H)
        return lax.dot_general(
            part[0][rows, :], ibuf[rows, :], (((0,), (0,)), ((), ())), preferred_element_type=F32
        )

    early = (coef_early, pl.ds(0, EARLY))
    late = (coef_late, pl.ds(EARLY, LATE))

    left_side = lax.broadcasted_iota(jnp.int32, (R, 128), 1) < 64

    def shard_of(d1, d2):
        rows = pl.ds(pl.multiple_of(slot_of(d1, d2) * H, 32), H)
        half = half_of(d1, d2)
        main = ip[rows, pl.ds(pl.multiple_of(half * 512, 512), 512)]
        low, high = ip[rows, pl.ds(1024, 128)][:R], ip[rows, pl.ds(1024, 128)][R:]
        rest = jnp.where(
            half == 0,
            jnp.where(left_side, low, pltpu.roll(high, 64, 1)),
            jnp.where(left_side, pltpu.roll(low, 64, 1), high),
        )
        return main, rest

    def send_shard(kind, key, place, shard, mains, rests_out, mains_in, rests_in, to):
        rows = pl.ds(place * H, H)
        mains[rows, :] = shard[0].astype(BF16)
        copy_of(kind, key, mains.at[rows, :], mains_in.at[rows, :], to).start()
        rows = blocks(place)
        rests_out[rows, :] = shard[1].astype(BF16)
        copy_of(kind, key, rests_out.at[rows, :], rests_in.at[rows, :], to).start()

    def add_shard(shard, place, mains_in, rests_in):
        return (
            shard[0] + mains_in[pl.ds(place * H, H), :].astype(F32),
            shard[1] + rests_in[blocks(place), :].astype(F32),
        )

    def send_b(d1, d2):
        to = {1: "bp", 2: "b2", 3: "bm"}[d2]
        shard = shard_of(d1, d2)
        send_shard("bo", ("bo", d1), 4 * d2 + d1, shard, b_main, b_rest, b_main_in, b_rest_in, to)

    def raw_inner(slot, carry):
        rows = pl.ds(pl.multiple_of(slot * H, 32), H)
        total = jnp.concatenate(rests(slot), axis=0) * ip[rows, pl.ds(1024, 128)]
        for q in range(4):
            product = rmain[q, rows, :].astype(F32) * ip[rows, pl.ds(256 * q, 256)]
            total = total + product[:, :128] + product[:, 128:]
        high = total.astype(BF16)
        low = (total - high.astype(F32)).astype(BF16)
        rows = pl.ds(pl.multiple_of(slot * 128, 128), H)
        inner_sums[rows, pl.ds(0, 128)] = high
        inner_sums[rows, pl.ds(128, 128)] = low
        return carry

    for d1 in range(4):
        for d2 in (1, 3):
            if d1 not in FORWARD or d2 != (1 if d1 in VIA_P else 3):
                got_i(("i", d1, d2))
    first, second = pl.ds(0, 4 * H), pl.ds(4 * H, 4 * H)
    normalised(0, 4)
    got("s early", tbuf.at[blocks(0, 5), :])
    coef_of(0, 4, early)
    ip[first, :] = image_sums(0, 4, early)
    late_t(3)
    late_t(5)
    for d1 in (0, 1):
        got_i(("i", d1, 2))
    normalised(4, 2)
    coef_of(4, 2, early)
    late_t(4)

    got("s late", tbuf.at[blocks(0, 3), :])
    coef_of(0, 4, late)
    ip[first, :] += image_sums(0, 4, late)
    for d1 in (2, 1, 3, 0):
        for d2 in (1, 3):
            send_b(d1, d2)
    coef_of(4, 2, late)
    for d1 in (2, 3):
        got_i(("i", d1, 2))
    normalised(6, 2)
    coef_of(6, 2, late)
    coef_of(6, 2, early)

    def inner_b():
        lax.fori_loop(0, 8, raw_inner, 0)
        along = lax.dot_general(
            jnp.ones((8, 256), BF16), inner_sums[...], (((1,), (1,)), ((), ())), preferred_element_type=F32
        )
        for slot in range(8):
            inner_slots[slot] = along[:, slot * 128:(slot + 1) * 128]
        for d2 in (1, 2, 3):
            for d1 in range(4):
                b_inner[4 * d2 + d1] = inner_slots[slot_of(d1, d2)]
            four = pl.ds(4 * d2, 4)
            to = {1: "bp", 2: "b2", 3: "bm"}[d2]
            copy_of("bi", "bi", b_inner.at[four], b_inner_in.at[four], to).start()

    def send_so(k):
        rows = blocks(k)
        sib_out[rows, :] = tp[blocks(OTHER[k]), :].astype(BF16)
        copy_of("so", ("so", k), sib_out.at[rows, :], sib_in.at[rows, :], "sib").start()

    tp[late[1], :] = text_sums(0, 8, late)
    for k in (4, 5, 3):
        send_so(k)
    tp[early[1], :] = text_sums(0, 8, early)
    for k in (6, 2, 7, 1, 0):
        send_so(k)
    def z_pass(*hops):
        for k, to, new in hops:
            got(("so", k), sib_in.at[blocks(k), :])
        for p in pieces:
            for k, to, new in hops:
                rows = rows_of(k, p)
                total = tp[rows_of(OWN[k], p), :] + sib_in[rows, :].astype(F32)
                if k not in (4, 5):
                    got(("zo", k, p), z_in.at[rows, :])
                    total = total + z_in[rows, :].astype(F32)
                z_out[rows, :] = total.astype(BF16)
                key = ("zo", new) if new in (0, 8) else ("zo", new, p)
                slot = 4 if new == 8 else new
                copy_of("zo", key, z_out.at[rows, :], z_in.at[rows_of(slot, p), :], to).start()

    z_pass((4, "zp", 3), (5, "zm", 6))
    ip[second, :] = image_sums(4, 4, early) + image_sums(4, 4, late)
    inner_b()
    for d1 in (2, 1, 3, 0):
        send_b(d1, 2)

    def b_sum(d1):
        got(("bo", d1), tbuf.at[blocks(0, 3), :])
        shard = shard_of(d1, 0)
        for d2 in (1, 2, 3):
            shard = add_shard(shard, 4 * d2 + d1, b_main_in, b_rest_in)
        return shard

    def send_a(d1, to):
        send_shard("ao", "ao", d1, b_sum(d1), a_main, a_rest, a_main_in, a_rest_in, to)

    def inner_sum(d1):
        return inner_slots[slot_of(d1, 0)] + b_inner_in[4 + d1] + b_inner_in[8 + d1] + b_inner_in[12 + d1]

    def inner_a():
        got("bi", b_inner.at[pl.ds(4, 12)])
        for d1, to in ((1, "ap"), (2, "a2"), (3, "am")):
            a_inner[d1] = inner_sum(d1)
            copy_of("ai", "ai", a_inner.at[d1], a_inner_in.at[d1], to).start()

    z_pass((3, "zp", 2), (6, "zm", 7))
    send_a(2, "a2")
    z_pass((2, "zp", 1), (7, "zm", 8))
    send_a(1, "ap")
    send_a(3, "am")
    inner_a()
    z_pass((1, "zp", 0))

    def back_norm(unit_rows, scale, inner, direction):
        return scale * (direction - unit_rows * inner)

    own_rows = pl.ds(4 * H, H)
    squares = jnp.concatenate(rests(4), axis=0) ** 2
    for q in range(4):
        part = rmain[q, own_rows, :].astype(F32)
        squares = squares + part[:, :128] ** 2 + part[:, 128:] ** 2
    scale_i = lax.rsqrt(jnp.sum(squares, axis=-1, keepdims=True) + 1e-06)
    unit_main = jnp.concatenate([rmain[2 * xh + i, own_rows, :].astype(F32) for i in (0, 1)], axis=1) * scale_i
    scale_rest = jnp.where(left_side, scale_i[:R], scale_i[R:])
    unit_rest = rrem[xh, blocks(4), :].astype(F32) * scale_rest
    got("ai", a_inner.at[pl.ds(1, 3)])
    along = inner_sum(0) + a_inner_in[1] + a_inner_in[2] + a_inner_in[3]
    inner_i = scale_i * jnp.transpose(jnp.broadcast_to(along[:1], (128, 128)))[:H, :1]
    inner_rest = jnp.where(left_side, inner_i[:R], inner_i[R:])

    shard = b_sum(0)
    got("ao", tbuf.at[blocks(0, 3), :])
    for d1 in (1, 2, 3):
        shard = add_shard(shard, d1, a_main_in, a_rest_in)
    grad = back_norm(unit_main, scale_i, inner_i, shard[0]).astype(BF16)
    g_main[0] = grad[:, :256]
    g_main[1] = grad[:, 256:]
    g_rest[...] = back_norm(unit_rest, scale_rest, inner_rest, shard[1]).astype(BF16)
    copy_of("g", "g", g_main.at[1 - c], g_main_in, "sib").start()
    copy_of("h", "g", g_rest, g_rest_in, "sib").start()

    def put_image(rows, main, rest):
        rest = rest.astype(F32)
        low = jnp.where(c == 0, rest[:, :32], rest[:, 32:64])
        high = jnp.where(c == 0, rest[:, 64:96], rest[:, 96:])
        oimg[rows, pl.ds(0, 256)] = main
        oimg[rows, pl.ds(256, 32)] = jnp.concatenate([low, high], axis=0).astype(BF16)

    put_image(here, g_main[c], g_rest[...])

    got(("so", 0), sib_in.at[blocks(0), :])
    got(("zo", 0), z_in.at[blocks(0), :])
    got(("zo", 8), z_in.at[blocks(4), :])
    direction = tp[blocks(0), :] + sib_in[blocks(0), :].astype(F32)
    direction = direction + z_in[blocks(0), :].astype(F32) + z_in[blocks(4), :].astype(F32)
    text_unit, text_scale = tunit[...], tscales[:, :1]
    text_inner = jnp.sum(text_unit * direction, axis=-1, keepdims=True)
    text_grad = back_norm(text_unit, text_scale, text_inner, direction)
    otxt[...] = jnp.concatenate([quarter(text_grad, j) for j in range(4)], axis=1).astype(BF16)

    left("x", rmain.at[0, pl.ds(0, H), :])
    left("y", xrem)
    left("t", tbuf.at[blocks(0, 7), :])
    left("s", tbuf.at[blocks(0, 8), :])
    left("i", ibuf.at[blocks(0, 15), :])
    left("so", sib_out)
    left("bo", tbuf.at[blocks(0, 12), :])
    left("zo", z_out.at[blocks(0, 7), :])
    left("ao", tbuf.at[blocks(0, 3), :])
    left("bi", b_inner.at[pl.ds(4, 12)])
    left("ai", a_inner.at[pl.ds(1, 3)])
    got("g", rrem.at[0, pl.ds(0, 5 * R), :])
    put_image(there, g_main_in[...], g_rest_in[...])
    left("g", g_main.at[0])
    left("h", g_rest)
    assert (len(send_ids), len(recv_ids)) == (SENDS, RECVS), (len(send_ids), len(recv_ids))


def hand_out(image_grad, text_grad, oimg, otxt, sems):
    copies = [
        pltpu.make_async_copy(image_grad, oimg, sems.at[0]),
        pltpu.make_async_copy(text_grad, otxt, sems.at[1]),
    ]
    for copy in copies:
        copy.start()
    for copy in copies:
        copy.wait()


def on_device(image_features, text_features):
    vmem = pltpu.VMEM
    image_grad, text_grad = pl.pallas_call(
        kernel,
        out_shape=(
            jax.ShapeDtypeStruct((4 * R, Q), BF16),
            jax.ShapeDtypeStruct((R, D), BF16),
        ),
        in_specs=[pl.BlockSpec(memory_space=pl.ANY)] * 2,
        out_specs=(pl.BlockSpec(memory_space=vmem), pl.BlockSpec(memory_space=vmem)),
        scratch_shapes=[
            vmem((4 * R, Q), BF16),
            vmem((R, 128), BF16),
            vmem((R, 128), BF16),
            vmem((4, N, 256), BF16),
            vmem((2, N // 2, 128), BF16),
            vmem((R, D), BF16),
            vmem((R, D), F32),
            vmem((R, 128), F32),
            vmem((N, D), BF16),
            vmem((N, D), BF16),
            vmem((N, EARLY), BF16),
            vmem((N, LATE), BF16),
            vmem((N, D), F32),
            vmem((N, D), F32),
            vmem((8 * R, D), BF16),
            vmem((8 * R, D), BF16),
            vmem((8 * R, D), BF16),
            vmem((8 * R, D), BF16),
            vmem((16 * H, 512), BF16),
            vmem((16 * R, 128), BF16),
            vmem((16 * H, 512), BF16),
            vmem((16 * R, 128), BF16),
            vmem((4 * H, 512), BF16),
            vmem((4 * R, 128), BF16),
            vmem((4 * H, 512), BF16),
            vmem((4 * R, 128), BF16),
            vmem((8 * 128, 256), BF16),
            vmem((8, 8, 128), F32),
            vmem((16, 8, 128), F32),
            vmem((16, 8, 128), F32),
            vmem((4, 8, 128), F32),
            vmem((4, 8, 128), F32),
            vmem((2, H, 256), BF16),
            vmem((R, 128), BF16),
            vmem((H, 256), BF16),
            vmem((R, 128), BF16),
            pltpu.SemaphoreType.DMA((SENDS,)),
            pltpu.SemaphoreType.DMA((RECVS,)),
            pltpu.SemaphoreType.DMA((3,)),
        ],
        compiler_params=pltpu.CompilerParams(
            collective_id=0, has_side_effects=True, vmem_limit_bytes=60 * 1024 * 1024
        ),
        cost_estimate=pl.CostEstimate(
            flops=6 * N * N * D, bytes_accessed=8 * R * D, transcendentals=N * N
        ),
    )(image_features, text_features)
    return pl.pallas_call(
        hand_out,
        out_shape=(
            jax.ShapeDtypeStruct((4 * R, Q), BF16),
            jax.ShapeDtypeStruct((R, D), BF16),
        ),
        in_specs=[pl.BlockSpec(memory_space=pltpu.VMEM)] * 2,
        out_specs=[pl.BlockSpec(memory_space=pltpu.HBM)] * 2,
        scratch_shapes=[pltpu.SemaphoreType.DMA((2,))],
    )(image_grad, text_grad)


def solution(mesh):
    placed = (P("loop", "grp"), P(("loop", "grp"), None))
    return jax.shard_map(
        on_device, mesh=mesh, in_specs=placed, out_specs=placed, check_vma=False
    )
```
